512 devices in a mesh: ctx: 128 (over z, x, core), ch: 4 (over y).
Axes of the slice: x: 4, y: 4, z: 16, core: 2. Of those that a mesh axis runs over, the one named last changes fastest.
Arguments:
- projected: bfloat16 [3, 16384, 4096], P(None, 'ctx', 'ch'), may hold values from -6 to 6
- short_filter: float32 [3, 3, 4096], P(None, None, 'ch'), may hold values from -3.5 to 3.5
- residues: float32 [4096, 16], P('ch'), may hold values from -5 to 5
- decays: float32 [4096, 16], P('ch'), as said below
- skip: float32 [4096], P('ch'), may hold values from -1 to 1
- out_weight: bfloat16 [4096, 4096], P('ch', 'ctx'), may hold values from -0.09375 to 0.09375
Outputs:
- result: bfloat16 [16384, 4096], P('ctx', 'ch')
The draws below stay inside these ranges and needn't reach their ends.
Inputs may be any that keep to these rules, and one draw needn't show every extreme that they name: `decays`: decay rates of the modal poles, at least 0.5 / 16384 and at most 1 / 32.
All inputs are finite; a program needn't handle non-finite values.
Results may differ from the reference program's by a relative error of at most 0.02.
Values may be sent and summed in bfloat16 or wider, within the bound.
A program may use at most 128 MiB of HBM per device.

```python
import math
import jax
import jax.numpy as jnp
from jax import lax

CW = 4096
DOUT = 4096
MODES = 16
SHORT = 3
TOKENS = 16384
N_CH = 4


def draw_decays(key, part):
    key = jax.random.fold_in(key, 7)
    lowest = math.log(0.5 / TOKENS)
    highest = math.log(1.0 / 32.0)
    return jnp.exp(jax.random.uniform(key, (CW, MODES), jnp.float32, lowest, highest))


def block_scale(rng, shape, shards, low, high):
    gain, own = 1.0, jax.random.fold_in(rng, 6)
    for position, parts in shards:
        draws = jnp.exp(jax.random.uniform(jax.random.fold_in(own, position), (parts,), jnp.float32, low / len(shards), high / len(shards)))
        gain = gain * jnp.repeat(draws, shape[position] // parts).reshape([-1 if axis == position else 1 for axis in range(len(shape))])
    return gain


def centred(own_key, shape, width, bound, cuts=(), held_as=jnp.bfloat16):
    array = width * jax.random.normal(own_key, shape, jnp.float32)
    if cuts:
        array = array * block_scale(own_key, shape, cuts, -0.22, 0.18)
    return jnp.clip(array, -bound, bound).astype(held_as)


def setup_inputs(seed: int = 0) -> dict:
    keys = jax.random.split(jax.random.key(seed), 7)
    projected = centred(keys[0], (3, TOKENS, CW), 1.0, 6.0, ((1, 128), (2, 4)))
    short_filter = centred(keys[1], (3, SHORT, CW), SHORT ** -0.5, 3.5, ((2, 4),), jnp.float32)
    residues = centred(keys[2], (CW, MODES), 0.35, 5.0, ((0, 4),), jnp.float32)
    decays = draw_decays(jax.random.fold_in(keys[6], 71), 0)
    skip = jnp.clip(jax.random.uniform(keys[4], (CW,), jnp.float32, -1.0, 1.0) * block_scale(keys[4], (CW,), ((0, 4),), -0.4, 0.0), -1.0, 1.0)
    out_weight = centred(keys[5], (CW, DOUT), CW ** -0.5, 0.09375, ((0, 4), (1, 128)))
    return dict(projected=projected, short_filter=short_filter, residues=residues, decays=decays, skip=skip, out_weight=out_weight)


def causal_short(sequence, filter_taps):
    count = filter_taps.shape[0]
    padded = jnp.pad(sequence, ((count - 1, 0), (0, 0)))
    total = jnp.zeros(sequence.shape, jnp.float32)
    for offset in range(count):
        begin = count - 1 - offset
        total = total + filter_taps[offset] * padded[begin:begin + sequence.shape[0]]
    return total

def long_block(operands):
    signal, residue_block, decay_block = operands
    times = jnp.arange(TOKENS).astype(jnp.float32)[:, None]

    def add_mode(mode, total):
        rate = lax.dynamic_index_in_dim(decay_block, mode, 1, False)
        amplitude = lax.dynamic_index_in_dim(residue_block, mode, 1, False) * jnp.sqrt(rate)
        return total + amplitude[None, :] * jnp.exp(-rate[None, :] * times)
    filter_taps = lax.fori_loop(0, MODES, add_mode, jnp.zeros(signal.shape, jnp.float32))
    spectrum = jnp.fft.rfft(filter_taps, 2 * TOKENS, axis=0) * jnp.fft.rfft(signal, 2 * TOKENS, axis=0)
    return jnp.fft.irfft(spectrum, 2 * TOKENS, axis=0)[:TOKENS]

def reference(projected, short_filter, residues, decays, skip, out_weight):
    shorts = [causal_short(projected[branch].astype(jnp.float32), short_filter[branch]) for branch in range(3)]
    mixed_in = (shorts[1] * shorts[2]).astype(jnp.bfloat16)
    group = CW // N_CH
    signal_groups = mixed_in.astype(jnp.float32).reshape(TOKENS, N_CH, group).transpose(1, 0, 2)
    convolved_groups = lax.map(long_block, (signal_groups, residues.reshape(N_CH, group, MODES), decays.reshape(N_CH, group, MODES)))
    convolved = convolved_groups.transpose(1, 0, 2).reshape(TOKENS, CW)
    gated = (shorts[0] * (convolved + skip * mixed_in.astype(jnp.float32))).astype(jnp.bfloat16)
    total = jnp.zeros((TOKENS, DOUT), jnp.float32)
    for quarter in range(N_CH):
        part_sum = jnp.dot(gated[:, quarter * group:(quarter + 1) * group], out_weight[quarter * group:(quarter + 1) * group], preferred_element_type=jnp.float32)
        total = total + part_sum.astype(jnp.bfloat16).astype(jnp.float32)
    return total.astype(jnp.bfloat16)
```

```python
import functools

import jax
import jax.numpy as jnp
from jax import lax
from jax.experimental import pallas as pl
from jax.experimental.pallas import tpu as pltpu
from jax.sharding import PartitionSpec as P

MESH = pl.DeviceIdType.MESH
F32 = jnp.float32
BF16 = jnp.bfloat16
STEPS = 16
MODES = 16
BLOCKS = 8


def unit_offsets():
    order = [0]
    for k in range(1, 8):
        order += [-k, k]
    return order + [-8]


def kernel(
    proj, sfilt, res, dec, skip, wt, out,
    x32, lam_t, al_t, l16_t, l32_t, l64_t, taps_t, sf_t, l128_t, l2048_t, pow_t, z_t, q_t, u_t, y_t, gt,
    hal_s, hal_r, sb, ab, tb, bb, cs, cr, wbuf, gb, ps, rb,
    h_s, h_r, w_s, w_r, x2_r, xf_r, ph_s, ph_r, g_s, g_r, rs_s, rs_r,
):
    ctx = lax.axis_index("ctx")
    y = lax.axis_index("ch")
    z = ctx // 8
    x = (ctx // 2) % 4
    c = ctx % 2
    grp = ctx // 16
    g = ctx % 16
    sib = z * 8 + x * 2 + (1 - c)

    def at(zz, xx):
        return (zz % 16) * 8 + (xx % 4) * 2 + c

    zr, zl = at(z + 1, x), at(z + 15, x)
    xr, xl, xo = at(z, x + 1), at(z, x + 3), at(z, x + 2)
    nxt, prv = (ctx + 1) % 128, (ctx + 127) % 128

    barrier = pltpu.get_barrier_semaphore()

    def greet(who, chan):
        pl.semaphore_signal(barrier, inc=1, device_id=(who, chan), device_id_type=MESH)

    for d in range(1, 16):
        greet(grp * 16 + (g + d) % 16, y)
    for d in range(1, 8):
        greet(((grp + d) % 8) * 16 + g, y)
    for d in range(1, 4):
        greet(ctx, (y + d) % 4)
        greet(sib, (y + d) % 4)
    for who in (zr, zl, nxt, prv):
        greet(who, y)
    greetings = 15 + 7 + 6 + 4

    for b in range(3):
        rows = proj[b, 112:128, :].astype(F32)
        for l in range(BLOCKS):
            hal_s[l, 2 * b : 2 * b + 2, :] = rows[14:16, l * 128 : (l + 1) * 128]
    for l in range(BLOCKS):
        hal_s[l, 6:8, :] = jnp.zeros((2, 128), F32)
    me_slot = z * 4 + x
    wbuf[me_slot] = wt[...]
    row = lax.broadcasted_iota(jnp.int32, (8, 128), 0)
    chunk_start = row.astype(F32) * float(STEPS)

    for l in range(BLOCKS):
        lanes = slice(l * 128, (l + 1) * 128)
        for b in range(3):
            x32[b, l] = proj[b, :, lanes].astype(F32)
        rate = dec[:, lanes]
        lam_t[l] = jnp.exp(-rate)
        l16_t[l] = jnp.exp(-16.0 * rate)
        l32_t[l] = jnp.exp(-32.0 * rate)
        l64_t[l] = jnp.exp(-64.0 * rate)
        hop = jnp.exp(-128.0 * rate)
        far = jnp.exp(-2048.0 * rate)
        for half in range(2):
            l128_t[half * 8 + l] = hop[half * 8 : half * 8 + 8]
            l2048_t[half * 8 + l] = far[half * 8 : half * 8 + 8]
        for b in range(3):
            sf_t[l, 3 * b : 3 * b + 3, :] = sfilt[b, :, lanes]

    pl.semaphore_wait(barrier, greetings)

    def halo_copy():
        return pltpu.make_async_remote_copy(
            src_ref=hal_s, dst_ref=hal_r, send_sem=h_s, recv_sem=h_r,
            device_id=(nxt, y), device_id_type=MESH)

    halo_copy().start()

    def push(slot, who, sem):
        pltpu.make_async_remote_copy(
            src_ref=wbuf.at[slot], dst_ref=wbuf.at[slot], send_sem=w_s, recv_sem=sem,
            device_id=(who, y), device_id_type=MESH).start()

    def landed(slot, sem):
        pltpu.make_async_copy(wbuf.at[slot], wbuf.at[slot], sem).wait()

    order = unit_offsets()

    def spread(slot, offset):
        n = order.index(offset)
        push(slot, xr, xf_r.at[0, n])
        push(slot, xl, xf_r.at[1, n])

    push(me_slot, zr, w_r.at[0, 0])
    push(me_slot, zl, w_r.at[1, 0])
    push(me_slot, xo, x2_r)
    spread(me_slot, 0)

    def slot_of(offset, xx):
        return ((z + offset + 16) % 16) * 4 + (xx % 4)

    def relay(k):
        for way, (sign, onward, last) in enumerate(((-1, zr, 8), (1, zl, 7))):
            if k > last:
                continue
            own, other = slot_of(sign * k, x), slot_of(sign * k, x + 2)
            landed(own, w_r.at[way, k - 1])
            if k < last:
                push(own, onward, w_r.at[way, k])
            spread(own, sign * k)
            landed(other, w_r.at[2 + way, k - 1])
            if k < last:
                push(other, onward, w_r.at[2 + way, k])

    def tables(l, carry):
        rate = dec_block(l)
        lam = lam_t[l]
        amp = res_block(l) * jnp.sqrt(rate)
        al_t[l] = amp * lam
        weight = amp
        rows = []
        for tap in range(STEPS):
            rows.append(jnp.sum(weight, axis=0, keepdims=True))
            weight = weight * lam
        rows[0] = rows[0] + skip[:, pl.ds(pl.multiple_of(l * 128, 128), 128)]
        for tap in range(STEPS):
            taps_t[l, tap : tap + 1, :] = rows[tap]
        for m in range(MODES):
            pow_t[l, m] = jnp.exp(-chunk_start * rate[m : m + 1, :])
        return carry

    def dec_block(l):
        return dec[:, pl.ds(pl.multiple_of(l * 128, 128), 128)]

    def res_block(l):
        return res[:, pl.ds(pl.multiple_of(l * 128, 128), 128)]

    lax.fori_loop(0, BLOCKS, tables, 0)

    other = slot_of(0, x + 2)
    landed(other, x2_r)
    push(other, zr, w_r.at[2, 0])
    push(other, zl, w_r.at[3, 0])

    halo_copy().wait()
    known = jnp.where(ctx == 0, 0.0, 1.0).astype(F32)
    keep1 = jnp.where(row >= 1, 1.0, 0.0).astype(F32)
    keep2 = jnp.where(row >= 2, 1.0, 0.0).astype(F32)
    keep4 = jnp.where(row >= 4, 1.0, 0.0).astype(F32)

    def states(l, carry):
        halo = hal_r[l] * known
        filt = sf_t[l]
        shorts = []
        for b in range(3):
            xs = [x32[b, l, pl.ds(j, 8, stride=STEPS), :] for j in range(STEPS)]
            before1 = jnp.where(row >= 1, pltpu.roll(xs[15], 1, 0), halo[2 * b + 1 : 2 * b + 2, :])
            before2 = jnp.where(row >= 1, pltpu.roll(xs[14], 1, 0), halo[2 * b : 2 * b + 1, :])
            line = [before2, before1] + xs
            f0, f1, f2 = (filt[3 * b + i : 3 * b + i + 1, :] for i in range(3))
            shorts.append([f0 * line[j + 2] + f1 * line[j + 1] + f2 * line[j] for j in range(STEPS)])
        us = [(shorts[1][j] * shorts[2][j]).astype(BF16).astype(F32) for j in range(STEPS)]
        for j in range(STEPS):
            q_t[l, j] = shorts[0][j]
            u_t[l, j] = us[j]
        lam, l16, l32, l64 = lam_t[l], l16_t[l], l32_t[l], l64_t[l]
        for m in range(MODES):
            rate = jnp.broadcast_to(lam[m : m + 1, :], (8, 128))
            end = us[0]
            for j in range(1, STEPS):
                end = end * rate + us[j]
            end = end + pltpu.roll(end, 1, 0) * (keep1 * l16[m : m + 1, :])
            end = end + pltpu.roll(end, 2, 0) * (keep2 * l32[m : m + 1, :])
            end = end + pltpu.roll(end, 4, 0) * (keep4 * l64[m : m + 1, :])
            z_t[l, m] = pltpu.roll(end, 1, 0) * keep1
            sb[(m // 8) * 8 + l, m % 8 : m % 8 + 1, :] = end[7:8, :]
        return carry

    lax.fori_loop(0, 4, states, 0)
    relay(1)
    lax.fori_loop(4, 8, states, 0)

    def member(d):
        return (g + d) % 16

    def to_member(src, dst, d, k):
        pltpu.make_async_remote_copy(
            src_ref=src, dst_ref=dst, send_sem=ph_s.at[k], recv_sem=ph_r.at[k],
            device_id=(grp * 16 + member(d), y), device_id_type=MESH).start()

    ab[g] = sb[g]

    def send_a(d, carry):
        to_member(sb.at[member(d)], ab.at[g], d, 0)
        return carry

    lax.fori_loop(1, 16, send_a, 0)

    def local(l, carry):
        us = [u_t[l, j] for j in range(STEPS)]
        taps = taps_t[l]
        rows = [jnp.broadcast_to(taps[t : t + 1, :], (8, 128)) for t in range(STEPS)]
        for j in range(STEPS):
            total = rows[0] * us[j]
            for t in range(1, j + 1):
                total = total + rows[t] * us[j - t]
            y_t[l, j] = total
        return carry

    relay(2)
    lax.fori_loop(0, 4, local, 0)

    def group_wait(buf, count, k):
        part = buf.at[pl.ds(0, count)]
        pltpu.make_async_copy(part, part, ph_r.at[k]).wait()

    group_wait(ab, 15, 0)
    hop = l128_t[g]
    total = ab[0]
    for h in range(1, 16):
        total = total * hop + ab[h]
    tb[...] = total

    def send_b(d, carry):
        pltpu.make_async_remote_copy(
            src_ref=tb, dst_ref=bb.at[d - 1], send_sem=ph_s.at[1], recv_sem=ph_r.at[1],
            device_id=(((grp + d) % 8) * 16 + g, y), device_id_type=MESH).start()
        return carry

    lax.fori_loop(1, 8, send_b, 0)
    relay(3)
    lax.fori_loop(4, 8, local, 0)
    group_wait(bb, 7, 1)
    far = l2048_t[g]
    state = jnp.zeros((8, 128), F32)
    for d in range(7, 0, -1):
        state = state * far + bb[d - 1] * jnp.where(grp >= d, 1.0, 0.0).astype(F32)
    for h in range(16):
        cs[h] = state
        state = state * hop + ab[h]
    cr[g] = cs[g]

    def send_c(d, carry):
        to_member(cs.at[member(d)], cr.at[g], d, 2)
        return carry

    lax.fori_loop(1, 16, send_c, 0)
    relay(4)
    group_wait(cr, 15, 2)

    def finish(l, carry):
        ys = [y_t[l, j] for j in range(STEPS)]
        lam, al = lam_t[l], al_t[l]
        tiles = [cr[l], cr[8 + l]]
        for m in range(MODES):
            rate = jnp.broadcast_to(lam[m : m + 1, :], (8, 128))
            start = z_t[l, m] + pow_t[l, m] * tiles[m // 8][m % 8 : m % 8 + 1, :]
            term = start * al[m : m + 1, :]
            for j in range(STEPS):
                ys[j] = ys[j] + term
                if j < STEPS - 1:
                    term = term * rate
        for j in range(STEPS):
            gt[l, pl.ds(j, 8, stride=STEPS), :] = q_t[l, j] * ys[j]
        return carry

    lax.fori_loop(0, 4, finish, 0)
    relay(5)
    lax.fori_loop(4, 8, finish, 0)
    for l in range(BLOCKS):
        gb[0, :, l * 128 : (l + 1) * 128] = gt[l].astype(BF16)
    gated = pltpu.make_async_remote_copy(
        src_ref=gb.at[0], dst_ref=gb.at[1], send_sem=g_s, recv_sem=g_r,
        device_id=(sib, y), device_id_type=MESH)
    gated.start()
    relay(6)
    gated.wait()

    def unit(n):
        offset = order[n]
        zq = (z + offset + 16) % 16
        landed(zq * 4 + (x + 3) % 4, xf_r.at[0, n])
        landed(zq * 4 + (x + 1) % 4, xf_r.at[1, n])
        weights = wbuf[pl.ds(zq * 4, 4)].reshape(128, 1024)
        part = lax.dot_general(
            gb[...].reshape(256, 1024), weights, (((1,), (1,)), ((), ())),
            preferred_element_type=F32).astype(BF16)
        ps[2 * n] = part[:128]
        ps[2 * n + 1] = part[128:]
        owner, place = zq // 4, zq % 4
        dy = (owner - y + 4) % 4
        pltpu.make_async_remote_copy(
            src_ref=ps.at[2 * n + 1], dst_ref=rb.at[dy, 1, place], send_sem=rs_s,
            recv_sem=rs_r.at[dy, 1, place], device_id=(sib, owner), device_id_type=MESH).start()

        @pl.when(dy != 0)
        def _():
            pltpu.make_async_remote_copy(
                src_ref=ps.at[2 * n], dst_ref=rb.at[dy, 0, place], send_sem=rs_s,
                recv_sem=rs_r.at[dy, 0, place], device_id=(ctx, owner), device_id_type=MESH).start()

        @pl.when(dy == 0)
        def _():
            rb[0, 0, place] = ps[2 * n]

    for n in range(0, 9):
        unit(n)
    relay(7)
    for n in range(9, 13):
        unit(n)
    relay(8)
    for n in range(13, 16):
        unit(n)

    lane = lax.broadcasted_iota(jnp.int32, (128, 128), 1) // 32
    for place in range(4):
        sums = []
        for core in range(2):
            rel = (core + c) % 2
            for dy in range(4):
                if core == 0:
                    for r in range(2):
                        if dy or r:
                            pltpu.make_async_copy(
                                rb.at[dy, r, place], rb.at[dy, r, place], rs_r.at[dy, r, place]).wait()
            acc = rb[0, rel, place].astype(F32)
            for dy in range(1, 4):
                acc = acc + rb[dy, rel, place].astype(F32)
            sums.append(acc)
        a, b = sums

        def pick(parts):
            return jnp.where(lane == 0, parts[0], jnp.where(lane == 1, parts[1], jnp.where(lane == 2, parts[2], parts[3])))

        a32, a64, a96 = (pltpu.roll(a, s, 1) for s in (32, 64, 96))
        b32, b64, b96 = (pltpu.roll(b, s, 1) for s in (32, 64, 96))
        out[:, place * 256 : place * 256 + 128] = pick((a, b32, a32, b64)).astype(BF16)
        out[:, place * 256 + 128 : place * 256 + 256] = pick((a64, b96, a96, b)).astype(BF16)

    part = wbuf.at[pl.ds(0, 63)]
    pltpu.make_async_copy(part, part, w_s).wait()
    for k, (buf, count) in enumerate(((sb, 15), (bb, 7), (cs, 15))):
        part = buf.at[pl.ds(0, count)]
        pltpu.make_async_copy(part, part, ph_s.at[k]).wait()
    part = ps.at[pl.ds(0, 28)]
    pltpu.make_async_copy(part, part, rs_s).wait()


def on_device(projected, short_filter, residues, decays, skip, out_weight):
    tile = (BLOCKS, MODES, 128)
    vm = pltpu.VMEM
    dma = pltpu.SemaphoreType.DMA
    return pl.pallas_call(
        kernel,
        out_shape=jax.ShapeDtypeStruct((128, 1024), BF16),
        in_specs=[pl.BlockSpec(memory_space=pltpu.VMEM)] * 6,
        out_specs=pl.BlockSpec(memory_space=pltpu.VMEM),
        scratch_shapes=[
            vm((3, 8, 128, 128), F32),
            vm(tile, F32), vm(tile, F32), vm(tile, F32), vm(tile, F32), vm(tile, F32),
            vm(tile, F32), vm(tile, F32),
            vm((16, 8, 128), F32), vm((16, 8, 128), F32),
            vm((8, 16, 8, 128), F32), vm((8, 16, 8, 128), F32),
            vm((8, 16, 8, 128), F32), vm((8, 16, 8, 128), F32), vm((8, 16, 8, 128), F32),
            vm((8, 128, 128), F32),
            vm((8, 8, 128), F32), vm((8, 8, 128), F32),
            vm((16, 8, 128), F32), vm((16, 8, 128), F32), vm((8, 128), F32),
            vm((8, 8, 128), F32), vm((16, 8, 128), F32), vm((16, 8, 128), F32),
            vm((64, 32, 1024), BF16), vm((2, 128, 1024), BF16),
            vm((32, 128, 128), BF16), vm((4, 2, 4, 128, 128), BF16),
            dma, dma, dma, dma((4, 8)), dma, dma((2, 16)), dma((3,)), dma((3,)),
            dma, dma, dma, dma((4, 2, 4)),
        ],
        compiler_params=pltpu.CompilerParams(
            collective_id=0, has_side_effects=True, vmem_limit_bytes=40 * 2**20),
        cost_estimate=pl.CostEstimate(flops=2**31, bytes_accessed=2**21, transcendentals=2**18),
        name="hyena",
    )(projected, short_filter, residues.T, decays.T, skip[None, :], out_weight.T)


def solution(mesh):
    return jax.shard_map(
        on_device,
        mesh=mesh,
        in_specs=(
            P(None, "ctx", "ch"), P(None, None, "ch"), P("ch", None), P("ch", None), P("ch"), P("ch", "ctx"),
        ),
        out_specs=P("ctx", "ch"),
        check_vma=False,
    )
```

```python
import functools

import jax
import jax.numpy as jnp
from jax import lax
from jax.experimental import pallas as pl
from jax.experimental.pallas import tpu as pltpu
from jax.sharding import PartitionSpec as P

MESH = pl.DeviceIdType.MESH
F32 = jnp.float32
BF16 = jnp.bfloat16
STEPS = 16
MODES = 16
OWN = 2
OTHER = 2
BLOCKS = 8


def unit_offsets():
    order = [0]
    for k in range(1, 8):
        order += [-k, k]
    return order + [-8]


def kernel(
    proj_h, sfilt_h, res_h, dec_h, skip_h, wt, out,
    proj, sfilt, res, dec, skip,
    x32, lam_t, al_t, l16_t, l32_t, l64_t, taps_t, sf_t, l128_t, l2048_t, pow_t, z_t, q_t, u_t, y_t, gt,
    hal_s, hal_r, sb, ab, tb, bb, cs, cr, wbuf, gb, ps, rb,
    in_s, h_s, h_r, w_s, w_r, x2_r, xf_r, ph_s, ph_r, g_s, g_r, rs_s, rs_r, st,
):
    ctx = lax.axis_index("ctx")
    y = lax.axis_index("ch")
    z = ctx // 8
    x = (ctx // 2) % 4
    c = ctx % 2
    grp = ctx // 16
    g = ctx % 16
    sib = z * 8 + x * 2 + (1 - c)

    def at(zz, xx):
        return (zz % 16) * 8 + (xx % 4) * 2 + c

    zr, zl = at(z + 1, x), at(z + 15, x)
    xr, xl, xo = at(z, x + 1), at(z, x + 3), at(z, x + 2)
    nxt, prv = (ctx + 1) % 128, (ctx + 127) % 128

    me_slot = z * 4 + x

    def fetch(k, src, dst):
        return pltpu.make_async_copy(src, dst, in_s.at[k])

    fetches = [
        fetch(0, proj_h, proj), fetch(1, wt, wbuf.at[me_slot]), fetch(2, dec_h, dec),
        fetch(3, sfilt_h, sfilt), fetch(4, res_h, res), fetch(5, skip_h, skip),
    ]
    for copy in fetches:
        copy.start()

    barrier = pltpu.get_barrier_semaphore()

    def greet(who, chan):
        pl.semaphore_signal(barrier, inc=1, device_id=(who, chan), device_id_type=MESH)

    beyond = at(z + 1 - 2 * ((z + 1) % 2) + 16, x)
    for who in (beyond, prv, at(z + 2, x), at(z + 14, x)):
        greet(who, y)
    for d in range(1, 16):
        greet(grp * 16 + (g + d) % 16, y)
    for d in range(1, 4):
        greet(ctx, (y + d) % 4)
        greet(sib, (y + d) % 4)
    greetings = 4 + 15 + 6

    fetches[0].wait()
    for b in range(3):
        rows = proj[b, 112:128, :].astype(F32)
        for l in range(BLOCKS):
            hal_s[l, 2 * b : 2 * b + 2, :] = rows[14:16, l * 128 : (l + 1) * 128]
    for l in range(BLOCKS):
        hal_s[l, 6:8, :] = jnp.zeros((2, 128), F32)
    row = lax.broadcasted_iota(jnp.int32, (8, 128), 0)
    chunk_start = row.astype(F32) * float(STEPS)
    fetches[1].wait()
    pl.semaphore_wait(barrier, greetings)

    def tell(k, far):
        for step in (far, 16 - far):
            pl.semaphore_signal(st.at[k], inc=1, device_id=(at(z + step, x), y), device_id_type=MESH)


    def halo_copy():
        return pltpu.make_async_remote_copy(
            src_ref=hal_s, dst_ref=hal_r, send_sem=h_s, recv_sem=h_r,
            device_id=(nxt, y), device_id_type=MESH)

    halo_copy().start()

    def rows_of(slot, part, parts):
        size = 32 // parts
        return wbuf.at[slot, pl.ds(part * size, size)]

    def push(slot, part, parts, who, sem):
        block = rows_of(slot, part, parts)
        pltpu.make_async_remote_copy(
            src_ref=block, dst_ref=block, send_sem=w_s, recv_sem=sem,
            device_id=(who, y), device_id_type=MESH).start()

    def landed(slot, part, parts, sem):
        block = rows_of(slot, part, parts)
        pltpu.make_async_copy(block, block, sem).wait()

    order = unit_offsets()

    def spread(slot, offset, part):
        n = order.index(offset)
        push(slot, part, OWN, xr, xf_r.at[0, n, part])
        push(slot, part, OWN, xl, xf_r.at[1, n, part])

    def slot_of(offset, xx):
        return ((z + offset + 16) % 16) * 4 + (xx % 4)

    ways = ((-1, zr, 8), (1, zl, 7))
    for part in range(OWN):
        for way in range(2):
            push(me_slot, part, OWN, ways[way][1], w_r.at[way, 0, part])
    for part in range(OTHER):
        push(me_slot, part, OTHER, xo, x2_r.at[part])
    for part in range(OWN):
        spread(me_slot, 0, part)
    tell(0, 2)

    def relay_own(k):
        for part in range(OWN):
            for way, (sign, onward, last) in enumerate(ways):
                if k <= last:
                    slot = slot_of(sign * k, x)
                    landed(slot, part, OWN, w_r.at[way, k - 1, part])
                    if k < last:
                        push(slot, part, OWN, onward, w_r.at[way, k, part])
            for sign, _, last in ways:
                if k <= last:
                    spread(slot_of(sign * k, x), sign * k, part)

    def relay_other(k):
        for part in range(OTHER):
            for way, (sign, onward, last) in enumerate(ways):
                if k <= last:
                    slot = slot_of(sign * k, x + 2)
                    landed(slot, part, OTHER, w_r.at[2 + way, k - 1, part])
                    if k < last:
                        push(slot, part, OTHER, onward, w_r.at[2 + way, k, part])

    for copy in fetches[2:]:
        copy.wait()
    for l in range(BLOCKS):
        lanes = slice(l * 128, (l + 1) * 128)
        for b in range(3):
            x32[b, l] = proj[b, :, lanes].astype(F32)
        rate = dec[:, lanes]
        lam_t[l] = jnp.exp(-rate)
        l16_t[l] = jnp.exp(-16.0 * rate)
        l32_t[l] = jnp.exp(-32.0 * rate)
        l64_t[l] = jnp.exp(-64.0 * rate)
        hop = jnp.exp(-128.0 * rate)
        far = jnp.exp(-2048.0 * rate)
        for half in range(2):
            l128_t[half * 8 + l] = hop[half * 8 : half * 8 + 8]
            l2048_t[half * 8 + l] = far[half * 8 : half * 8 + 8]
        for b in range(3):
            sf_t[l, 3 * b : 3 * b + 3, :] = sfilt[b, :, lanes]

    def tables(l, carry):
        rate = dec_block(l)
        lam = lam_t[l]
        amp = res_block(l) * jnp.sqrt(rate)
        al_t[l] = amp * lam
        weight = amp
        rows = []
        for tap in range(STEPS):
            rows.append(jnp.sum(weight, axis=0, keepdims=True))
            weight = weight * lam
        rows[0] = rows[0] + skip[:, pl.ds(pl.multiple_of(l * 128, 128), 128)]
        for tap in range(STEPS):
            taps_t[l, tap : tap + 1, :] = rows[tap]
        for m in range(MODES):
            pow_t[l, m] = jnp.exp(-chunk_start * rate[m : m + 1, :])
        return carry

    def dec_block(l):
        return dec[:, pl.ds(pl.multiple_of(l * 128, 128), 128)]

    def res_block(l):
        return res[:, pl.ds(pl.multiple_of(l * 128, 128), 128)]

    other = slot_of(0, x + 2)
    for part in range(OTHER):
        landed(other, part, OTHER, x2_r.at[part])
        push(other, part, OTHER, zr, w_r.at[2, 0, part])
        push(other, part, OTHER, zl, w_r.at[3, 0, part])

    halo_copy().wait()
    known = jnp.where(ctx == 0, 0.0, 1.0).astype(F32)
    keep1 = jnp.where(row >= 1, 1.0, 0.0).astype(F32)
    keep2 = jnp.where(row >= 2, 1.0, 0.0).astype(F32)
    keep4 = jnp.where(row >= 4, 1.0, 0.0).astype(F32)

    def states(l, carry):
        halo = hal_r[l] * known
        filt = sf_t[l]
        shorts = []
        for b in range(3):
            xs = [x32[b, l, pl.ds(j, 8, stride=STEPS), :] for j in range(STEPS)]
            before1 = jnp.where(row >= 1, pltpu.roll(xs[15], 1, 0), halo[2 * b + 1 : 2 * b + 2, :])
            before2 = jnp.where(row >= 1, pltpu.roll(xs[14], 1, 0), halo[2 * b : 2 * b + 1, :])
            line = [before2, before1] + xs
            f0, f1, f2 = (filt[3 * b + i : 3 * b + i + 1, :] for i in range(3))
            shorts.append([f0 * line[j + 2] + f1 * line[j + 1] + f2 * line[j] for j in range(STEPS)])
        us = [(shorts[1][j] * shorts[2][j]).astype(BF16).astype(F32) for j in range(STEPS)]
        for j in range(STEPS):
            q_t[l, j] = shorts[0][j]
            u_t[l, j] = us[j]
        lam, l16, l32, l64 = lam_t[l], l16_t[l], l32_t[l], l64_t[l]
        for m in range(MODES):
            rate = jnp.broadcast_to(lam[m : m + 1, :], (8, 128))
            end = us[0]
            for j in range(1, STEPS):
                end = end * rate + us[j]
            end = end + pltpu.roll(end, 1, 0) * (keep1 * l16[m : m + 1, :])
            end = end + pltpu.roll(end, 2, 0) * (keep2 * l32[m : m + 1, :])
            end = end + pltpu.roll(end, 4, 0) * (keep4 * l64[m : m + 1, :])
            z_t[l, m] = pltpu.roll(end, 1, 0) * keep1
            sb[(m // 8) * 8 + l, m % 8 : m % 8 + 1, :] = end[7:8, :]
        return carry

    lax.fori_loop(0, 4, states, 0)
    relay_own(1)
    pl.semaphore_wait(st.at[0], 2)
    tell(1, 4)
    lax.fori_loop(4, 8, states, 0)

    def member(d):
        return (g + d) % 16

    def to_member(src, dst, d, k):
        pltpu.make_async_remote_copy(
            src_ref=src, dst_ref=dst, send_sem=ph_s.at[k], recv_sem=ph_r.at[k],
            device_id=(grp * 16 + member(d), y), device_id_type=MESH).start()

    ab[g] = sb[g]

    def send_a(d, carry):
        to_member(sb.at[member(d)], ab.at[g], d, 0)
        return carry

    lax.fori_loop(1, 16, send_a, 0)

    def local(l, carry):
        us = [u_t[l, j] for j in range(STEPS)]
        taps = taps_t[l]
        rows = [jnp.broadcast_to(taps[t : t + 1, :], (8, 128)) for t in range(STEPS)]
        for j in range(STEPS):
            total = rows[0] * us[j]
            for t in range(1, j + 1):
                total = total + rows[t] * us[j - t]
            y_t[l, j] = total
        return carry

    relay_other(1)
    lax.fori_loop(0, BLOCKS, tables, 0)
    relay_own(2)
    lax.fori_loop(0, 8, local, 0)
    relay_other(2)

    def group_wait(buf, count, k):
        part = buf.at[pl.ds(0, count)]
        pltpu.make_async_copy(part, part, ph_r.at[k]).wait()

    group_wait(ab, 15, 0)
    hop = l128_t[g]
    total = ab[0]
    for h in range(1, 16):
        total = total * hop + ab[h]
    tb[...] = total

    def send_b(d, carry):
        pltpu.make_async_remote_copy(
            src_ref=tb, dst_ref=bb.at[d - 1], send_sem=ph_s.at[1], recv_sem=ph_r.at[1],
            device_id=(((grp + d) % 8) * 16 + g, y), device_id_type=MESH).start()
        return carry

    pl.semaphore_wait(st.at[1], 2)
    lax.fori_loop(1, 8, send_b, 0)
    relay_own(3)
    relay_other(3)
    relay_own(4)
    relay_other(4)
    group_wait(bb, 7, 1)
    far = l2048_t[g]
    state = jnp.zeros((8, 128), F32)
    for d in range(7, 0, -1):
        state = state * far + bb[d - 1] * jnp.where(grp >= d, 1.0, 0.0).astype(F32)
    for h in range(16):
        cs[h] = state
        state = state * hop + ab[h]
    cr[g] = cs[g]

    def send_c(d, carry):
        to_member(cs.at[member(d)], cr.at[g], d, 2)
        return carry

    lax.fori_loop(1, 16, send_c, 0)
    relay_own(5)
    relay_other(5)
    group_wait(cr, 15, 2)

    def finish(l, carry):
        ys = [y_t[l, j] for j in range(STEPS)]
        lam, al = lam_t[l], al_t[l]
        tiles = [cr[l], cr[8 + l]]
        for m in range(MODES):
            rate = jnp.broadcast_to(lam[m : m + 1, :], (8, 128))
            start = z_t[l, m] + pow_t[l, m] * tiles[m // 8][m % 8 : m % 8 + 1, :]
            term = start * al[m : m + 1, :]
            for j in range(STEPS):
                ys[j] = ys[j] + term
                if j < STEPS - 1:
                    term = term * rate
        for j in range(STEPS):
            gt[l, pl.ds(j, 8, stride=STEPS), :] = q_t[l, j] * ys[j]
        return carry

    def gated(half):
        lanes = pl.ds(half * 512, 512)
        return pltpu.make_async_remote_copy(
            src_ref=gb.at[0, :, lanes], dst_ref=gb.at[1, :, lanes], send_sem=g_s.at[half],
            recv_sem=g_r.at[half], device_id=(sib, y), device_id_type=MESH)

    for half in range(2):
        lax.fori_loop(4 * half, 4 * half + 4, finish, 0)
        for l in range(4 * half, 4 * half + 4):
            gb[0, :, l * 128 : (l + 1) * 128] = gt[l].astype(BF16)
        gated(half).start()
        if half == 0:
            relay_own(6)
    for half in range(2):
        gated(half).wait()
    relay_other(6)

    def units(*offsets):
        weights = []
        for offset in offsets:
            n = order.index(offset)
            zq = (z + offset + 16) % 16
            for part in range(OWN):
                landed(zq * 4 + (x + 3) % 4, part, OWN, xf_r.at[0, n, part])
                landed(zq * 4 + (x + 1) % 4, part, OWN, xf_r.at[1, n, part])
            weights.append(wbuf[pl.ds(zq * 4, 4)].reshape(128, 1024))
        part = lax.dot_general(
            gb[...].reshape(256, 1024), jnp.concatenate(weights, axis=0), (((1,), (1,)), ((), ())),
            preferred_element_type=F32).astype(BF16)
        for i, offset in enumerate(offsets):
            n = order.index(offset)
            zq = (z + offset + 16) % 16
            ps[2 * n] = part[:128, i * 128 : (i + 1) * 128]
            ps[2 * n + 1] = part[128:, i * 128 : (i + 1) * 128]
            ship(n, zq)

    def ship(n, zq):
        owner, place = zq // 4, zq % 4
        dy = (owner - y + 4) % 4
        pltpu.make_async_remote_copy(
            src_ref=ps.at[2 * n + 1], dst_ref=rb.at[dy, 1, place], send_sem=rs_s,
            recv_sem=rs_r.at[dy, 1, place], device_id=(sib, owner), device_id_type=MESH).start()

        @pl.when(dy != 0)
        def _():
            pltpu.make_async_remote_copy(
                src_ref=ps.at[2 * n], dst_ref=rb.at[dy, 0, place], send_sem=rs_s,
                recv_sem=rs_r.at[dy, 0, place], device_id=(ctx, owner), device_id_type=MESH).start()

        @pl.when(dy == 0)
        def _():
            rb[0, 0, place] = ps[2 * n]

    units(0, 4)
    units(-4, 1)
    units(5, -3)
    relay_own(7)
    units(-1, 3)
    units(-5, 2)
    relay_other(7)
    units(6, -2)
    relay_own(8)
    units(-6, 7)
    relay_other(8)
    units(-7)
    units(-8)

    lane = lax.broadcasted_iota(jnp.int32, (128, 128), 1) // 32
    for place in range(4):
        sums = []
        for core in range(2):
            rel = (core + c) % 2
            for dy in range(4):
                if core == 0:
                    for r in range(2):
                        if dy or r:
                            pltpu.make_async_copy(
                                rb.at[dy, r, place], rb.at[dy, r, place], rs_r.at[dy, r, place]).wait()
            acc = rb[0, rel, place].astype(F32)
            for dy in range(1, 4):
                acc = acc + rb[dy, rel, place].astype(F32)
            sums.append(acc)
        a, b = sums

        def pick(parts):
            return jnp.where(lane == 0, parts[0], jnp.where(lane == 1, parts[1], jnp.where(lane == 2, parts[2], parts[3])))

        a32, a64, a96 = (pltpu.roll(a, s, 1) for s in (32, 64, 96))
        b32, b64, b96 = (pltpu.roll(b, s, 1) for s in (32, 64, 96))
        out[:, place * 256 : place * 256 + 128] = pick((a, b32, a32, b64)).astype(BF16)
        out[:, place * 256 + 128 : place * 256 + 256] = pick((a64, b96, a96, b)).astype(BF16)

    part = wbuf.at[pl.ds(0, 63)]
    pltpu.make_async_copy(part, part, w_s).wait()
    for k, (buf, count) in enumerate(((sb, 15), (bb, 7), (cs, 15))):
        part = buf.at[pl.ds(0, count)]
        pltpu.make_async_copy(part, part, ph_s.at[k]).wait()
    part = ps.at[pl.ds(0, 28)]
    pltpu.make_async_copy(part, part, rs_s).wait()


def on_device(projected, short_filter, residues, decays, skip, out_weight):
    tile = (BLOCKS, MODES, 128)
    vm = pltpu.VMEM
    dma = pltpu.SemaphoreType.DMA
    return pl.pallas_call(
        kernel,
        out_shape=jax.ShapeDtypeStruct((128, 1024), BF16),
        in_specs=[pl.BlockSpec(memory_space=pl.ANY)] * 6,
        out_specs=pl.BlockSpec(memory_space=pltpu.VMEM),
        scratch_shapes=[
            vm((3, 128, 1024), BF16), vm((3, 3, 1024), F32), vm((16, 1024), F32), vm((16, 1024), F32), vm((1, 1024), F32),
            vm((3, 8, 128, 128), F32),
            vm(tile, F32), vm(tile, F32), vm(tile, F32), vm(tile, F32), vm(tile, F32),
            vm(tile, F32), vm(tile, F32),
            vm((16, 8, 128), F32), vm((16, 8, 128), F32),
            vm((8, 16, 8, 128), F32), vm((8, 16, 8, 128), F32),
            vm((8, 16, 8, 128), F32), vm((8, 16, 8, 128), F32), vm((8, 16, 8, 128), F32),
            vm((8, 128, 128), F32),
            vm((8, 8, 128), F32), vm((8, 8, 128), F32),
            vm((16, 8, 128), F32), vm((16, 8, 128), F32), vm((8, 128), F32),
            vm((8, 8, 128), F32), vm((16, 8, 128), F32), vm((16, 8, 128), F32),
            vm((64, 32, 1024), BF16), vm((2, 128, 1024), BF16),
            vm((32, 128, 128), BF16), vm((4, 2, 4, 128, 128), BF16),
            dma((6,)), dma, dma, dma, dma((4, 8, 2)), dma((2,)), dma((2, 16, 2)), dma((3,)), dma((3,)),
            dma((2,)), dma((2,)), dma, dma((4, 2, 4)), pltpu.SemaphoreType.REGULAR((2,)),
        ],
        compiler_params=pltpu.CompilerParams(
            collective_id=0, has_side_effects=True, vmem_limit_bytes=63 * 2**20),
        cost_estimate=pl.CostEstimate(flops=2**31, bytes_accessed=2**21, transcendentals=2**18),
        name="hyena",
    )(projected, short_filter, residues.T, decays.T, skip[None, :], out_weight.T)


def solution(mesh):
    return jax.shard_map(
        on_device,
        mesh=mesh,
        in_specs=(
            P(None, "ctx", "ch"), P(None, None, "ch"), P("ch", None), P("ch", None), P("ch"), P("ch", "ctx"),
        ),
        out_specs=P("ctx", "ch"),
        check_vma=False,
    )
```

```python
import functools

import jax
import jax.numpy as jnp
from jax import lax
from jax.experimental import pallas as pl
from jax.experimental.pallas import tpu as pltpu
from jax.sharding import PartitionSpec as P

MESH = pl.DeviceIdType.MESH
F32 = jnp.float32
BF16 = jnp.bfloat16
STEPS = 16
MODES = 16
OWN = 2
OTHER = 2
BLOCKS = 8


TURNS = (
    (-5, 4, 0, -4, 5, 1, -6, 6, -3, 2, -7, 7, -2, 3, -1, -8),
    (4, -5, 0, -4, 5, 1, -6, 6, 3, -1, 7, -7, -3, 2, -2, -8),
    (5, -4, 0, 4, -5, 1, 6, -6, 3, -1, 7, -7, -3, 2, -2, -8),
    (5, -4, 4, 0, -5, -1, 6, -6, 3, -2, 7, -7, 2, -3, 1, -8),
)


def kernel(
    proj_h, sfilt_h, res_h, dec_h, skip_h, wt, out,
    proj, sfilt, res, dec, skip,
    x32, lam_t, al_t, l16_t, l32_t, l64_t, taps_t, sf_t, l128_t, l2048_t, pow_t, z_t, q_t, u_t, y_t, gt,
    hal_s, hal_r, sb, ab, tb, bb, cs, cr, wbuf, gb, ps, rb,
    in_s, h_s, h_r, w_s, w_r, x2_r, xf_r, ph_s, ph_r, g_s, g_r, rs_s, rs_r, st,
):
    ctx = lax.axis_index("ctx")
    y = lax.axis_index("ch")
    z = ctx // 8
    x = (ctx // 2) % 4
    c = ctx % 2
    grp = ctx // 16
    g = ctx % 16
    sib = z * 8 + x * 2 + (1 - c)

    def at(zz, xx):
        return (zz % 16) * 8 + (xx % 4) * 2 + c

    zr, zl = at(z + 1, x), at(z + 15, x)
    xr, xl, xo = at(z, x + 1), at(z, x + 3), at(z, x + 2)
    nxt, prv = (ctx + 1) % 128, (ctx + 127) % 128

    me_slot = z * 4 + x

    barrier = pltpu.get_barrier_semaphore()
    twin = at(z + 1 - 2 * (z % 2) + 16, x)
    near = (zr, zl, xr, xl, xo, sib, prv, twin + 1 - 2 * c, at(z + 2, x), at(z + 14, x))
    for who in near:
        pl.semaphore_signal(barrier, inc=1, device_id=(who, y), device_id_type=MESH)
    for d in range(1, 4):
        pl.semaphore_signal(barrier, inc=1, device_id=(ctx, (y + d) % 4), device_id_type=MESH)

    def fetch(k, src, dst):
        return pltpu.make_async_copy(src, dst, in_s.at[k])

    fetches = [
        fetch(0, proj_h, proj), fetch(1, wt, wbuf.at[me_slot]), fetch(2, dec_h, dec),
        fetch(3, sfilt_h, sfilt), fetch(4, res_h, res), fetch(5, skip_h, skip),
    ]
    for copy in fetches:
        copy.start()

    row = lax.broadcasted_iota(jnp.int32, (8, 128), 0)
    chunk_start = row.astype(F32) * float(STEPS)
    pl.semaphore_wait(barrier, len(near) + 3)

    def tell(k, partners):
        for who in partners:
            pl.semaphore_signal(st.at[k], inc=1, device_id=(who, y), device_id_type=MESH)

    def halo_copy():
        return pltpu.make_async_remote_copy(
            src_ref=hal_s, dst_ref=hal_r, send_sem=h_s, recv_sem=h_r,
            device_id=(nxt, y), device_id_type=MESH)

    def rows_of(slot, part, parts):
        size = 32 // parts
        return wbuf.at[slot, pl.ds(part * size, size)]

    def push(slot, part, parts, who, sem):
        block = rows_of(slot, part, parts)
        pltpu.make_async_remote_copy(
            src_ref=block, dst_ref=block, send_sem=w_s, recv_sem=sem,
            device_id=(who, y), device_id_type=MESH).start()

    def landed(slot, part, parts, sem):
        block = rows_of(slot, part, parts)
        pltpu.make_async_copy(block, block, sem).wait()

    def spread(slot, offset, part):
        n = offset % 16
        push(slot, part, OWN, xr, xf_r.at[0, n, part])
        push(slot, part, OWN, xl, xf_r.at[1, n, part])

    def slot_of(offset, xx):
        return ((z + offset + 16) % 16) * 4 + (xx % 4)

    ways = ((-1, zr), (1, zl))

    def push_mine(part, parts, who, sem):
        size = 32 // parts
        pltpu.make_async_remote_copy(
            src_ref=wt.at[pl.ds(part * size, size)], dst_ref=rows_of(me_slot, part, parts),
            send_sem=w_s, recv_sem=sem, device_id=(who, y), device_id_type=MESH).start()

    for part in range(OWN):
        for way in range(2):
            push_mine(part, OWN, ways[way][1], w_r.at[way, 0, part])
    for part in range(OTHER):
        push_mine(part, OTHER, xo, x2_r.at[part])
    tell(0, (sib, xr, xl, xo, at(z + 2, x), at(z + 14, x)))

    fetches[0].wait()
    for b in range(3):
        rows = proj[b, 112:128, :].astype(F32)
        for l in range(BLOCKS):
            hal_s[l, 2 * b : 2 * b + 2, :] = rows[14:16, l * 128 : (l + 1) * 128]
    for l in range(BLOCKS):
        hal_s[l, 6:8, :] = jnp.zeros((2, 128), F32)
    halo_copy().start()
    for part in range(OWN):
        push_mine(part, OWN, xr, xf_r.at[0, 0, part])
        push_mine(part, OWN, xl, xf_r.at[1, 0, part])

    def relay_own(k):
        for part in range(OWN):
            for way, (sign, onward) in enumerate(ways):
                last = 8 if part % 2 == way else 7
                if k <= last:
                    slot = slot_of(sign * k, x)
                    landed(slot, part, OWN, w_r.at[way, k - 1, part])
                    if k < last:
                        push(slot, part, OWN, onward, w_r.at[way, k, part])
            for way, (sign, _) in enumerate(ways):
                if k <= (8 if part % 2 == way else 7):
                    spread(slot_of(sign * k, x), sign * k, part)

    def relay_other(k):
        for part in range(OTHER):
            for way, (sign, onward) in enumerate(ways):
                last = 8 if part % 2 == way else 7
                if k <= last:
                    slot = slot_of(sign * k, x + 2)
                    landed(slot, part, OTHER, w_r.at[2 + way, k - 1, part])
                    if k < last:
                        push(slot, part, OTHER, onward, w_r.at[2 + way, k, part])

    for copy in fetches[1:]:
        copy.wait()
    for l in range(BLOCKS):
        lanes = slice(l * 128, (l + 1) * 128)
        for b in range(3):
            x32[b, l] = proj[b, :, lanes].astype(F32)
        rate = dec[:, lanes]
        lam_t[l] = jnp.exp(-rate)
        l16_t[l] = jnp.exp(-16.0 * rate)
        l32_t[l] = jnp.exp(-32.0 * rate)
        l64_t[l] = jnp.exp(-64.0 * rate)
        hop = jnp.exp(-128.0 * rate)
        far = jnp.exp(-2048.0 * rate)
        for half in range(2):
            l128_t[half * 8 + l] = hop[half * 8 : half * 8 + 8]
            l2048_t[half * 8 + l] = far[half * 8 : half * 8 + 8]
        for b in range(3):
            sf_t[l, 3 * b : 3 * b + 3, :] = sfilt[b, :, lanes]

    def tables(l, carry):
        rate = dec_block(l)
        lam = lam_t[l]
        amp = res_block(l) * jnp.sqrt(rate)
        al_t[l] = amp * lam
        weight = amp
        rows = []
        for tap in range(STEPS):
            rows.append(jnp.sum(weight, axis=0, keepdims=True))
            weight = weight * lam
        rows[0] = rows[0] + skip[:, pl.ds(pl.multiple_of(l * 128, 128), 128)]
        for tap in range(STEPS):
            taps_t[l, tap : tap + 1, :] = rows[tap]
        for m in range(MODES):
            pow_t[l, m] = jnp.exp(-chunk_start * rate[m : m + 1, :])
        return carry

    def dec_block(l):
        return dec[:, pl.ds(pl.multiple_of(l * 128, 128), 128)]

    def res_block(l):
        return res[:, pl.ds(pl.multiple_of(l * 128, 128), 128)]

    other = slot_of(0, x + 2)
    for part in range(OTHER):
        landed(other, part, OTHER, x2_r.at[part])
        push(other, part, OTHER, zr, w_r.at[2, 0, part])
        push(other, part, OTHER, zl, w_r.at[3, 0, part])

    halo_copy().wait()
    known = jnp.where(ctx == 0, 0.0, 1.0).astype(F32)
    keep1 = jnp.where(row >= 1, 1.0, 0.0).astype(F32)
    keep2 = jnp.where(row >= 2, 1.0, 0.0).astype(F32)
    keep4 = jnp.where(row >= 4, 1.0, 0.0).astype(F32)

    def states(l, carry):
        halo = hal_r[l] * known
        filt = sf_t[l]
        shorts = []
        for b in range(3):
            xs = [x32[b, l, pl.ds(j, 8, stride=STEPS), :] for j in range(STEPS)]
            before1 = jnp.where(row >= 1, pltpu.roll(xs[15], 1, 0), halo[2 * b + 1 : 2 * b + 2, :])
            before2 = jnp.where(row >= 1, pltpu.roll(xs[14], 1, 0), halo[2 * b : 2 * b + 1, :])
            line = [before2, before1] + xs
            f0, f1, f2 = (filt[3 * b + i : 3 * b + i + 1, :] for i in range(3))
            shorts.append([f0 * line[j + 2] + f1 * line[j + 1] + f2 * line[j] for j in range(STEPS)])
        us = [(shorts[1][j] * shorts[2][j]).astype(BF16).astype(F32) for j in range(STEPS)]
        for j in range(STEPS):
            q_t[l, j] = shorts[0][j]
            u_t[l, j] = us[j]
        lam, l16, l32, l64 = lam_t[l], l16_t[l], l32_t[l], l64_t[l]
        for m in range(MODES):
            rate = jnp.broadcast_to(lam[m : m + 1, :], (8, 128))
            end = us[0]
            for j in range(1, STEPS):
                end = end * rate + us[j]
            end = end + pltpu.roll(end, 1, 0) * (keep1 * l16[m : m + 1, :])
            end = end + pltpu.roll(end, 2, 0) * (keep2 * l32[m : m + 1, :])
            end = end + pltpu.roll(end, 4, 0) * (keep4 * l64[m : m + 1, :])
            z_t[l, m] = pltpu.roll(end, 1, 0) * keep1
            sb[(m // 8) * 8 + l, m % 8 : m % 8 + 1, :] = end[7:8, :]
        return carry

    lax.fori_loop(0, 4, states, 0)
    relay_own(1)
    pl.semaphore_wait(st.at[0], 6)
    tell(1, (at(z + 4, x), at(z + 12, x)))
    lax.fori_loop(4, 8, states, 0)

    def member(d):
        return (g + d) % 16

    def to_member(src, dst, d, k):
        pltpu.make_async_remote_copy(
            src_ref=src, dst_ref=dst, send_sem=ph_s.at[k], recv_sem=ph_r.at[k],
            device_id=(grp * 16 + member(d), y), device_id_type=MESH).start()

    ab[g] = sb[g]

    members = (4, 12, 5, 11, 3, 13, 8, 7, 9, 6, 10, 2, 14, 15, 1)
    for d in members:
        to_member(sb.at[member(d)], ab.at[g], d, 0)

    def local(l, carry):
        us = [u_t[l, j] for j in range(STEPS)]
        taps = taps_t[l]
        rows = [jnp.broadcast_to(taps[t : t + 1, :], (8, 128)) for t in range(STEPS)]
        for j in range(STEPS):
            total = rows[0] * us[j]
            for t in range(1, j + 1):
                total = total + rows[t] * us[j - t]
            y_t[l, j] = total
        return carry

    relay_other(1)
    lax.fori_loop(0, BLOCKS, tables, 0)
    relay_own(2)
    lax.fori_loop(0, 8, local, 0)
    relay_other(2)

    def group_wait(buf, count, k):
        part = buf.at[pl.ds(0, count)]
        pltpu.make_async_copy(part, part, ph_r.at[k]).wait()

    group_wait(ab, 15, 0)
    hop = l128_t[g]
    total = ab[0]
    for h in range(1, 16):
        total = total * hop + ab[h]
    tb[...] = total

    pl.semaphore_wait(st.at[1], 2)
    for d in (4, 3, 5, 2, 6, 1, 7):
        pltpu.make_async_remote_copy(
            src_ref=tb, dst_ref=bb.at[d - 1], send_sem=ph_s.at[1], recv_sem=ph_r.at[1],
            device_id=(((grp + d) % 8) * 16 + g, y), device_id_type=MESH).start()
    relay_own(3)
    relay_other(3)
    relay_own(4)
    relay_other(4)
    group_wait(bb, 7, 1)
    far = l2048_t[g]
    state = jnp.zeros((8, 128), F32)
    for d in range(7, 0, -1):
        state = state * far + bb[d - 1] * jnp.where(grp >= d, 1.0, 0.0).astype(F32)
    for h in range(16):
        cs[h] = state
        state = state * hop + ab[h]
    cr[g] = cs[g]

    for d in members:
        to_member(cs.at[member(d)], cr.at[g], d, 2)
    relay_own(5)
    relay_other(5)
    group_wait(cr, 15, 2)

    def finish(l, carry):
        ys = [y_t[l, j] for j in range(STEPS)]
        lam, al = lam_t[l], al_t[l]
        tiles = [cr[l], cr[8 + l]]
        for m in range(MODES):
            rate = jnp.broadcast_to(lam[m : m + 1, :], (8, 128))
            start = z_t[l, m] + pow_t[l, m] * tiles[m // 8][m % 8 : m % 8 + 1, :]
            term = start * al[m : m + 1, :]
            for j in range(STEPS):
                ys[j] = ys[j] + term
                if j < STEPS - 1:
                    term = term * rate
        for j in range(STEPS):
            gt[l, pl.ds(j, 8, stride=STEPS), :] = q_t[l, j] * ys[j]
        return carry

    def gated(half):
        lanes = pl.ds(half * 512, 512)
        return pltpu.make_async_remote_copy(
            src_ref=gb.at[0, :, lanes], dst_ref=gb.at[1, :, lanes], send_sem=g_s.at[half],
            recv_sem=g_r.at[half], device_id=(sib, y), device_id_type=MESH)

    for half in range(2):
        lax.fori_loop(4 * half, 4 * half + 4, finish, 0)
        for l in range(4 * half, 4 * half + 4):
            gb[0, :, l * 128 : (l + 1) * 128] = gt[l].astype(BF16)
        gated(half).start()
        if half == 0:
            relay_own(6)

    def distance(turn):
        a, b, c_, d = (row[turn] % 16 for row in TURNS)
        r = z % 4
        return jnp.where(r == 0, a, jnp.where(r == 1, b, jnp.where(r == 2, c_, d)))

    def units(*turns, cores=(0, 1)):
        weights = []
        for turn in turns:
            n = distance(turn)
            zq = (z + n) % 16
            if 0 in cores:
                for part in range(OWN):
                    landed(zq * 4 + (x + 3) % 4, part, OWN, xf_r.at[0, n, part])
                    landed(zq * 4 + (x + 1) % 4, part, OWN, xf_r.at[1, n, part])
            weights.append(wbuf[pl.ds(zq * 4, 4)].reshape(128, 1024))
        tokens = gb[cores[0] : cores[-1] + 1].reshape(128 * len(cores), 1024)
        part = lax.dot_general(
            tokens, jnp.concatenate(weights, axis=0), (((1,), (1,)), ((), ())),
            preferred_element_type=F32).astype(BF16)
        for i, turn in enumerate(turns):
            for k, core in enumerate(cores):
                ps[2 * turn + core] = part[k * 128 : (k + 1) * 128, i * 128 : (i + 1) * 128]
                ship(turn, (z + distance(turn)) % 16, core)

    def ship(n, zq, core):
        owner, place = zq // 4, zq % 4
        dy = (owner - y + 4) % 4

        def copy(who):
            pltpu.make_async_remote_copy(
                src_ref=ps.at[2 * n + core], dst_ref=rb.at[dy, core, place], send_sem=rs_s,
                recv_sem=rs_r.at[dy, core, place], device_id=(who, owner), device_id_type=MESH).start()

        if core == 1:
            copy(sib)
        else:
            @pl.when(dy != 0)
            def _():
                copy(ctx)

            @pl.when(dy == 0)
            def _():
                rb[0, 0, place] = ps[2 * n]

    units(0, 1, cores=(0,))
    units(2, 3, cores=(0,))
    for half in range(2):
        gated(half).wait()
    units(0, 1, cores=(1,))
    units(2, 3, cores=(1,))
    relay_other(6)
    units(4, 5)
    relay_own(7)
    units(6, 7)
    relay_other(7)
    units(8, 9)
    relay_own(8)
    units(10, 11)
    units(12, 13)
    units(14)
    relay_other(8)
    units(15)

    lane = lax.broadcasted_iota(jnp.int32, (128, 128), 1) // 32
    first = (4 * y - z + 16) % 16
    for turn in range(4):
        place = jnp.where(first < 8, turn, 3 - turn)
        sums = []
        for core in range(2):
            rel = (core + c) % 2
            for dy in range(4):
                if core == 0:
                    for r in range(2):
                        if dy or r:
                            pltpu.make_async_copy(
                                rb.at[dy, r, place], rb.at[dy, r, place], rs_r.at[dy, r, place]).wait()
            acc = rb[0, rel, place].astype(F32)
            for dy in range(1, 4):
                acc = acc + rb[dy, rel, place].astype(F32)
            sums.append(acc)
        a, b = sums

        def pick(parts):
            return jnp.where(lane == 0, parts[0], jnp.where(lane == 1, parts[1], jnp.where(lane == 2, parts[2], parts[3])))

        a32, a64, a96 = (pltpu.roll(a, s, 1) for s in (32, 64, 96))
        b32, b64, b96 = (pltpu.roll(b, s, 1) for s in (32, 64, 96))
        at0 = pl.multiple_of(place * 256, 128)
        out[:, pl.ds(at0, 128)] = pick((a, b32, a32, b64)).astype(BF16)
        out[:, pl.ds(pl.multiple_of(at0 + 128, 128), 128)] = pick((a64, b96, a96, b)).astype(BF16)

    part = wbuf.at[pl.ds(0, 63)]
    pltpu.make_async_copy(part, part, w_s).wait()
    for k, (buf, count) in enumerate(((sb, 15), (bb, 7), (cs, 15))):
        part = buf.at[pl.ds(0, count)]
        pltpu.make_async_copy(part, part, ph_s.at[k]).wait()
    part = ps.at[pl.ds(0, 28)]
    pltpu.make_async_copy(part, part, rs_s).wait()


def on_device(projected, short_filter, residues, decays, skip, out_weight):
    tile = (BLOCKS, MODES, 128)
    vm = pltpu.VMEM
    dma = pltpu.SemaphoreType.DMA
    return pl.pallas_call(
        kernel,
        out_shape=jax.ShapeDtypeStruct((128, 1024), BF16),
        in_specs=[pl.BlockSpec(memory_space=pl.ANY)] * 6,
        out_specs=pl.BlockSpec(memory_space=pltpu.VMEM),
        scratch_shapes=[
            vm((3, 128, 1024), BF16), vm((3, 3, 1024), F32), vm((16, 1024), F32), vm((16, 1024), F32), vm((1, 1024), F32),
            vm((3, 8, 128, 128), F32),
            vm(tile, F32), vm(tile, F32), vm(tile, F32), vm(tile, F32), vm(tile, F32),
            vm(tile, F32), vm(tile, F32),
            vm((16, 8, 128), F32), vm((16, 8, 128), F32),
            vm((8, 16, 8, 128), F32), vm((8, 16, 8, 128), F32),
            vm((8, 16, 8, 128), F32), vm((8, 16, 8, 128), F32), vm((8, 16, 8, 128), F32),
            vm((8, 128, 128), F32),
            vm((8, 8, 128), F32), vm((8, 8, 128), F32),
            vm((16, 8, 128), F32), vm((16, 8, 128), F32), vm((8, 128), F32),
            vm((8, 8, 128), F32), vm((16, 8, 128), F32), vm((16, 8, 128), F32),
            vm((64, 32, 1024), BF16), vm((2, 128, 1024), BF16),
            vm((32, 128, 128), BF16), vm((4, 2, 4, 128, 128), BF16),
            dma((6,)), dma, dma, dma, dma((4, 8, 2)), dma((2,)), dma((2, 16, 2)), dma((3,)), dma((3,)),
            dma((2,)), dma((2,)), dma, dma((4, 2, 4)), pltpu.SemaphoreType.REGULAR((2,)),
        ],
        compiler_params=pltpu.CompilerParams(
            collective_id=0, has_side_effects=True, vmem_limit_bytes=63 * 2**20),
        cost_estimate=pl.CostEstimate(flops=2**31, bytes_accessed=2**21, transcendentals=2**18),
        name="hyena",
    )(projected, short_filter, residues.T, decays.T, skip[None, :], out_weight.T)


def solution(mesh):
    return jax.shard_map(
        on_device,
        mesh=mesh,
        in_specs=(
            P(None, "ctx", "ch"), P(None, None, "ch"), P("ch", None), P("ch", None), P("ch"), P("ch", "ctx"),
        ),
        out_specs=P("ctx", "ch"),
        check_vma=False,
    )
```

```python
import functools

import jax
import jax.numpy as jnp
from jax import lax
from jax.experimental import pallas as pl
from jax.experimental.pallas import tpu as pltpu
from jax.sharding import PartitionSpec as P

MESH = pl.DeviceIdType.MESH
F32 = jnp.float32
BF16 = jnp.bfloat16
STEPS = 16
MODES = 16
OWN = 2
OTHER = 2
BLOCKS = 8


TURNS = (
    (-5, 4, 0, -4, 5, 1, -6, 6, -3, 2, -7, 7, -2, 3, -1, -8),
    (4, -5, 0, -4, 5, 1, -6, 6, 3, -1, 7, -7, -3, 2, -2, -8),
    (5, -4, 0, 4, -5, 1, 6, -6, 3, -1, 7, -7, -3, 2, -2, -8),
    (5, -4, 4, 0, -5, -1, 6, -6, 3, -2, 7, -7, 2, -3, 1, -8),
)


def kernel(
    proj_h, sfilt_h, res_h, dec_h, skip_h, wt, out,
    proj, sfilt, res, dec, skip,
    x32, lam_t, al_t, l16_t, l32_t, l64_t, taps_t, sf_t, l128_t, l2048_t, pow_t, z_t, q_t, u_t, y_t, gt,
    hal_s, hal_r, sb, ab, tb, bb, cs, cr, wbuf, gb, ps, rb,
    in_s, h_s, h_r, w_s, w_r, x2_r, xf_r, ph_s, ph_r, g_s, g_r, rs_s, rs_r, st,
):
    ctx = lax.axis_index("ctx")
    y = lax.axis_index("ch")
    z = ctx // 8
    x = (ctx // 2) % 4
    c = ctx % 2
    grp = ctx // 16
    g = ctx % 16
    sib = z * 8 + x * 2 + (1 - c)

    def at(zz, xx):
        return (zz % 16) * 8 + (xx % 4) * 2 + c

    zr, zl = at(z + 1, x), at(z + 15, x)
    xr, xl, xo = at(z, x + 1), at(z, x + 3), at(z, x + 2)
    nxt, prv = (ctx + 1) % 128, (ctx + 127) % 128

    me_slot = z * 4 + x

    barrier = pltpu.get_barrier_semaphore()
    twin = at(z + 1 - 2 * (z % 2) + 16, x)
    near = (zr, zl, xr, xl, xo, sib, prv, twin + 1 - 2 * c, at(z + 2, x), at(z + 14, x))
    for who in near:
        pl.semaphore_signal(barrier, inc=1, device_id=(who, y), device_id_type=MESH)
    for d in range(1, 4):
        pl.semaphore_signal(barrier, inc=1, device_id=(ctx, (y + d) % 4), device_id_type=MESH)

    def fetch(k, src, dst):
        return pltpu.make_async_copy(src, dst, in_s.at[k])

    fetches = [
        fetch(0, proj_h, proj), fetch(1, wt, wbuf.at[me_slot]), fetch(2, dec_h, dec),
        fetch(3, sfilt_h, sfilt), fetch(4, res_h, res), fetch(5, skip_h, skip),
    ]
    for copy in fetches:
        copy.start()

    row = lax.broadcasted_iota(jnp.int32, (8, 128), 0)
    chunk_start = row.astype(F32) * float(STEPS)
    pl.semaphore_wait(barrier, len(near) + 3)

    def tell(k, partners):
        for who in partners:
            pl.semaphore_signal(st.at[k], inc=1, device_id=(who, y), device_id_type=MESH)

    def halo_copy():
        return pltpu.make_async_remote_copy(
            src_ref=hal_s, dst_ref=hal_r, send_sem=h_s, recv_sem=h_r,
            device_id=(nxt, y), device_id_type=MESH)

    def rows_of(slot, part, parts):
        size = 32 // parts
        return wbuf.at[slot, pl.ds(part * size, size)]

    def push(slot, part, parts, who, sem):
        block = rows_of(slot, part, parts)
        pltpu.make_async_remote_copy(
            src_ref=block, dst_ref=block, send_sem=w_s, recv_sem=sem,
            device_id=(who, y), device_id_type=MESH).start()

    def landed(slot, part, parts, sem):
        block = rows_of(slot, part, parts)
        pltpu.make_async_copy(block, block, sem).wait()

    def spread(slot, offset, part):
        n = offset % 16
        push(slot, part, OWN, xr, xf_r.at[0, n, part])
        push(slot, part, OWN, xl, xf_r.at[1, n, part])

    def slot_of(offset, xx):
        return ((z + offset + 16) % 16) * 4 + (xx % 4)

    ways = ((-1, zr), (1, zl))

    def push_mine(part, parts, who, sem):
        size = 32 // parts
        pltpu.make_async_remote_copy(
            src_ref=wt.at[pl.ds(part * size, size)], dst_ref=rows_of(me_slot, part, parts),
            send_sem=w_s, recv_sem=sem, device_id=(who, y), device_id_type=MESH).start()

    for part in range(OWN):
        for way in range(2):
            push_mine(part, OWN, ways[way][1], w_r.at[way, 0, part])
    for part in range(OTHER):
        push_mine(part, OTHER, xo, x2_r.at[part])
    tell(0, (sib, xr, xl, xo, at(z + 2, x), at(z + 14, x)))

    fetches[0].wait()
    for b in range(3):
        rows = proj[b, 112:128, :].astype(F32)
        for l in range(BLOCKS):
            hal_s[l, 2 * b : 2 * b + 2, :] = rows[14:16, l * 128 : (l + 1) * 128]
    for l in range(BLOCKS):
        hal_s[l, 6:8, :] = jnp.zeros((2, 128), F32)
    halo_copy().start()

    def relay_own(k):
        for part in range(OWN):
            for way, (sign, onward) in enumerate(ways):
                last = 8 if part % 2 == way else 7
                if k <= last:
                    slot = slot_of(sign * k, x)
                    landed(slot, part, OWN, w_r.at[way, k - 1, part])
                    if k < last:
                        push(slot, part, OWN, onward, w_r.at[way, k, part])
            for way, (sign, _) in enumerate(ways):
                if k <= (8 if part % 2 == way else 7):
                    spread(slot_of(sign * k, x), sign * k, part)

    def relay_other(k):
        for part in range(OTHER):
            for way, (sign, onward) in enumerate(ways):
                last = 8 if part % 2 == way else 7
                if k <= last:
                    slot = slot_of(sign * k, x + 2)
                    landed(slot, part, OTHER, w_r.at[2 + way, k - 1, part])
                    if k < last:
                        push(slot, part, OTHER, onward, w_r.at[2 + way, k, part])

    for copy in fetches[1:]:
        copy.wait()
    for l in range(BLOCKS):
        lanes = slice(l * 128, (l + 1) * 128)
        for b in range(3):
            x32[b, l] = proj[b, :, lanes].astype(F32)
        rate = dec[:, lanes]
        lam_t[l] = jnp.exp(-rate)
        l16_t[l] = jnp.exp(-16.0 * rate)
        l32_t[l] = jnp.exp(-32.0 * rate)
        l64_t[l] = jnp.exp(-64.0 * rate)
        hop = jnp.exp(-128.0 * rate)
        far = jnp.exp(-2048.0 * rate)
        for half in range(2):
            l128_t[half * 8 + l] = hop[half * 8 : half * 8 + 8]
            l2048_t[half * 8 + l] = far[half * 8 : half * 8 + 8]
        for b in range(3):
            sf_t[l, 3 * b : 3 * b + 3, :] = sfilt[b, :, lanes]

    def tables(l, carry):
        rate = dec_block(l)
        lam = lam_t[l]
        amp = res_block(l) * jnp.sqrt(rate)
        al_t[l] = amp * lam
        weight = amp
        rows = []
        for tap in range(STEPS):
            rows.append(jnp.sum(weight, axis=0, keepdims=True))
            weight = weight * lam
        rows[0] = rows[0] + skip[:, pl.ds(pl.multiple_of(l * 128, 128), 128)]
        for tap in range(STEPS):
            taps_t[l, tap : tap + 1, :] = rows[tap]
        for m in range(MODES):
            pow_t[l, m] = jnp.exp(-chunk_start * rate[m : m + 1, :])
        return carry

    def dec_block(l):
        return dec[:, pl.ds(pl.multiple_of(l * 128, 128), 128)]

    def res_block(l):
        return res[:, pl.ds(pl.multiple_of(l * 128, 128), 128)]

    other = slot_of(0, x + 2)
    for part in range(OTHER):
        landed(other, part, OTHER, x2_r.at[part])
        push(other, part, OTHER, zr, w_r.at[2, 0, part])
        push(other, part, OTHER, zl, w_r.at[3, 0, part])

    halo_copy().wait()
    known = jnp.where(ctx == 0, 0.0, 1.0).astype(F32)
    keep1 = jnp.where(row >= 1, 1.0, 0.0).astype(F32)
    keep2 = jnp.where(row >= 2, 1.0, 0.0).astype(F32)
    keep4 = jnp.where(row >= 4, 1.0, 0.0).astype(F32)

    def states(l, carry):
        halo = hal_r[l] * known
        filt = sf_t[l]
        shorts = []
        for b in range(3):
            xs = [x32[b, l, pl.ds(j, 8, stride=STEPS), :] for j in range(STEPS)]
            before1 = jnp.where(row >= 1, pltpu.roll(xs[15], 1, 0), halo[2 * b + 1 : 2 * b + 2, :])
            before2 = jnp.where(row >= 1, pltpu.roll(xs[14], 1, 0), halo[2 * b : 2 * b + 1, :])
            line = [before2, before1] + xs
            f0, f1, f2 = (filt[3 * b + i : 3 * b + i + 1, :] for i in range(3))
            shorts.append([f0 * line[j + 2] + f1 * line[j + 1] + f2 * line[j] for j in range(STEPS)])
        us = [(shorts[1][j] * shorts[2][j]).astype(BF16).astype(F32) for j in range(STEPS)]
        for j in range(STEPS):
            q_t[l, j] = shorts[0][j]
            u_t[l, j] = us[j]
        lam, l16, l32, l64 = lam_t[l], l16_t[l], l32_t[l], l64_t[l]
        for m in range(MODES):
            rate = jnp.broadcast_to(lam[m : m + 1, :], (8, 128))
            end = us[0]
            for j in range(1, STEPS):
                end = end * rate + us[j]
            end = end + pltpu.roll(end, 1, 0) * (keep1 * l16[m : m + 1, :])
            end = end + pltpu.roll(end, 2, 0) * (keep2 * l32[m : m + 1, :])
            end = end + pltpu.roll(end, 4, 0) * (keep4 * l64[m : m + 1, :])
            z_t[l, m] = pltpu.roll(end, 1, 0) * keep1
            sb[(m // 8) * 8 + l, m % 8 : m % 8 + 1, :] = end[7:8, :]
        return carry

    lax.fori_loop(0, 4, states, 0)
    relay_own(1)
    pl.semaphore_wait(st.at[0], 6)
    tell(1, (at(z + 4, x), at(z + 12, x)))
    lax.fori_loop(4, 8, states, 0)

    def member(d):
        return (g + d) % 16

    def to_member(src, dst, d, k):
        pltpu.make_async_remote_copy(
            src_ref=src, dst_ref=dst, send_sem=ph_s.at[k], recv_sem=ph_r.at[k],
            device_id=(grp * 16 + member(d), y), device_id_type=MESH).start()

    ab[g] = sb[g]

    members = (4, 12, 5, 11, 3, 13, 8, 7, 9, 6, 10, 2, 14, 15, 1)
    for d in members:
        to_member(sb.at[member(d)], ab.at[g], d, 0)

    def local(l, carry):
        us = [u_t[l, j] for j in range(STEPS)]
        taps = taps_t[l]
        rows = [jnp.broadcast_to(taps[t : t + 1, :], (8, 128)) for t in range(STEPS)]
        for j in range(STEPS):
            total = rows[0] * us[j]
            for t in range(1, j + 1):
                total = total + rows[t] * us[j - t]
            y_t[l, j] = total
        return carry

    relay_other(1)
    lax.fori_loop(0, BLOCKS, tables, 0)
    relay_own(2)
    lax.fori_loop(0, 8, local, 0)
    relay_other(2)

    def group_wait(buf, count, k):
        part = buf.at[pl.ds(0, count)]
        pltpu.make_async_copy(part, part, ph_r.at[k]).wait()

    group_wait(ab, 15, 0)
    hop = l128_t[g]
    total = ab[0]
    for h in range(1, 16):
        total = total * hop + ab[h]
    tb[...] = total

    pl.semaphore_wait(st.at[1], 2)
    for d in (4, 3, 5, 2, 6, 1, 7):
        pltpu.make_async_remote_copy(
            src_ref=tb, dst_ref=bb.at[d - 1], send_sem=ph_s.at[1], recv_sem=ph_r.at[1],
            device_id=(((grp + d) % 8) * 16 + g, y), device_id_type=MESH).start()
    for part in range(OWN):
        push_mine(part, OWN, xr, xf_r.at[0, 0, part])
        push_mine(part, OWN, xl, xf_r.at[1, 0, part])
    relay_own(3)
    relay_other(3)
    relay_own(4)
    relay_other(4)
    group_wait(bb, 7, 1)
    far = l2048_t[g]
    state = jnp.zeros((8, 128), F32)
    for d in range(7, 0, -1):
        state = state * far + bb[d - 1] * jnp.where(grp >= d, 1.0, 0.0).astype(F32)
    for h in range(16):
        cs[h] = state
        state = state * hop + ab[h]
    cr[g] = cs[g]

    for d in members:
        to_member(cs.at[member(d)], cr.at[g], d, 2)
    relay_own(5)
    relay_other(5)
    group_wait(cr, 15, 2)

    def finish(l, carry):
        ys = [y_t[l, j] for j in range(STEPS)]
        lam, al = lam_t[l], al_t[l]
        tiles = [cr[l], cr[8 + l]]
        for m in range(MODES):
            rate = jnp.broadcast_to(lam[m : m + 1, :], (8, 128))
            start = z_t[l, m] + pow_t[l, m] * tiles[m // 8][m % 8 : m % 8 + 1, :]
            term = start * al[m : m + 1, :]
            for j in range(STEPS):
                ys[j] = ys[j] + term
                if j < STEPS - 1:
                    term = term * rate
        for j in range(STEPS):
            gt[l, pl.ds(j, 8, stride=STEPS), :] = q_t[l, j] * ys[j]
        return carry

    def gated(half):
        lanes = pl.ds(half * 512, 512)
        return pltpu.make_async_remote_copy(
            src_ref=gb.at[0, :, lanes], dst_ref=gb.at[1, :, lanes], send_sem=g_s.at[half],
            recv_sem=g_r.at[half], device_id=(sib, y), device_id_type=MESH)

    for half in range(2):
        lax.fori_loop(4 * half, 4 * half + 4, finish, 0)
        for l in range(4 * half, 4 * half + 4):
            gb[0, :, l * 128 : (l + 1) * 128] = gt[l].astype(BF16)
        gated(half).start()
        if half == 0:
            relay_own(6)

    def distance(turn):
        a, b, c_, d = (row[turn] % 16 for row in TURNS)
        r = z % 4
        return jnp.where(r == 0, a, jnp.where(r == 1, b, jnp.where(r == 2, c_, d)))

    def units(*turns, cores=(0, 1)):
        weights = []
        for turn in turns:
            n = distance(turn)
            zq = (z + n) % 16
            if 0 in cores:
                for part in range(OWN):
                    landed(zq * 4 + (x + 3) % 4, part, OWN, xf_r.at[0, n, part])
                    landed(zq * 4 + (x + 1) % 4, part, OWN, xf_r.at[1, n, part])
            weights.append(wbuf[pl.ds(zq * 4, 4)].reshape(128, 1024))
        tokens = gb[cores[0] : cores[-1] + 1].reshape(128 * len(cores), 1024)
        part = lax.dot_general(
            tokens, jnp.concatenate(weights, axis=0), (((1,), (1,)), ((), ())),
            preferred_element_type=F32).astype(BF16)
        for i, turn in enumerate(turns):
            for k, core in enumerate(cores):
                ps[2 * turn + core] = part[k * 128 : (k + 1) * 128, i * 128 : (i + 1) * 128]
                ship(turn, (z + distance(turn)) % 16, core)

    def ship(n, zq, core):
        owner, place = zq // 4, zq % 4
        dy = (owner - y + 4) % 4

        def copy(who):
            pltpu.make_async_remote_copy(
                src_ref=ps.at[2 * n + core], dst_ref=rb.at[dy, core, place], send_sem=rs_s,
                recv_sem=rs_r.at[dy, core, place], device_id=(who, owner), device_id_type=MESH).start()

        if core == 1:
            copy(sib)
        else:
            @pl.when(dy != 0)
            def _():
                copy(ctx)

            @pl.when(dy == 0)
            def _():
                rb[0, 0, place] = ps[2 * n]

    units(0, 1, cores=(0,))
    units(2, 3, cores=(0,))
    for half in range(2):
        gated(half).wait()
    units(0, 1, cores=(1,))
    units(2, 3, cores=(1,))
    relay_other(6)
    units(4, 5)
    relay_own(7)
    units(6, 7)
    relay_other(7)
    units(8, 9)
    relay_own(8)
    units(10, 11)
    units(12, 13)
    units(14)
    relay_other(8)
    units(15)

    lane = lax.broadcasted_iota(jnp.int32, (128, 128), 1) // 32
    first = (4 * y - z + 16) % 16
    for turn in range(4):
        place = jnp.where(first < 8, turn, 3 - turn)
        sums = []
        for core in range(2):
            rel = (core + c) % 2
            for dy in range(4):
                if core == 0:
                    for r in range(2):
                        if dy or r:
                            pltpu.make_async_copy(
                                rb.at[dy, r, place], rb.at[dy, r, place], rs_r.at[dy, r, place]).wait()
            acc = rb[0, rel, place].astype(F32)
            for dy in range(1, 4):
                acc = acc + rb[dy, rel, place].astype(F32)
            sums.append(acc)
        a, b = sums

        def pick(parts):
            return jnp.where(lane == 0, parts[0], jnp.where(lane == 1, parts[1], jnp.where(lane == 2, parts[2], parts[3])))

        a32, a64, a96 = (pltpu.roll(a, s, 1) for s in (32, 64, 96))
        b32, b64, b96 = (pltpu.roll(b, s, 1) for s in (32, 64, 96))
        at0 = pl.multiple_of(place * 256, 128)
        out[:, pl.ds(at0, 128)] = pick((a, b32, a32, b64)).astype(BF16)
        out[:, pl.ds(pl.multiple_of(at0 + 128, 128), 128)] = pick((a64, b96, a96, b)).astype(BF16)

    part = wbuf.at[pl.ds(0, 63)]
    pltpu.make_async_copy(part, part, w_s).wait()
    for k, (buf, count) in enumerate(((sb, 15), (bb, 7), (cs, 15))):
        part = buf.at[pl.ds(0, count)]
        pltpu.make_async_copy(part, part, ph_s.at[k]).wait()
    part = ps.at[pl.ds(0, 28)]
    pltpu.make_async_copy(part, part, rs_s).wait()


def on_device(projected, short_filter, residues, decays, skip, out_weight):
    tile = (BLOCKS, MODES, 128)
    vm = pltpu.VMEM
    dma = pltpu.SemaphoreType.DMA
    return pl.pallas_call(
        kernel,
        out_shape=jax.ShapeDtypeStruct((128, 1024), BF16),
        in_specs=[pl.BlockSpec(memory_space=pl.ANY)] * 6,
        out_specs=pl.BlockSpec(memory_space=pltpu.VMEM),
        scratch_shapes=[
            vm((3, 128, 1024), BF16), vm((3, 3, 1024), F32), vm((16, 1024), F32), vm((16, 1024), F32), vm((1, 1024), F32),
            vm((3, 8, 128, 128), F32),
            vm(tile, F32), vm(tile, F32), vm(tile, F32), vm(tile, F32), vm(tile, F32),
            vm(tile, F32), vm(tile, F32),
            vm((16, 8, 128), F32), vm((16, 8, 128), F32),
            vm((8, 16, 8, 128), F32), vm((8, 16, 8, 128), F32),
            vm((8, 16, 8, 128), F32), vm((8, 16, 8, 128), F32), vm((8, 16, 8, 128), F32),
            vm((8, 128, 128), F32),
            vm((8, 8, 128), F32), vm((8, 8, 128), F32),
            vm((16, 8, 128), F32), vm((16, 8, 128), F32), vm((8, 128), F32),
            vm((8, 8, 128), F32), vm((16, 8, 128), F32), vm((16, 8, 128), F32),
            vm((64, 32, 1024), BF16), vm((2, 128, 1024), BF16),
            vm((32, 128, 128), BF16), vm((4, 2, 4, 128, 128), BF16),
            dma((6,)), dma, dma, dma, dma((4, 8, 2)), dma((2,)), dma((2, 16, 2)), dma((3,)), dma((3,)),
            dma((2,)), dma((2,)), dma, dma((4, 2, 4)), pltpu.SemaphoreType.REGULAR((2,)),
        ],
        compiler_params=pltpu.CompilerParams(
            collective_id=0, has_side_effects=True, vmem_limit_bytes=63 * 2**20),
        cost_estimate=pl.CostEstimate(flops=2**31, bytes_accessed=2**21, transcendentals=2**18),
        name="hyena",
    )(projected, short_filter, residues.T, decays.T, skip[None, :], out_weight.T)


def solution(mesh):
    return jax.shard_map(
        on_device,
        mesh=mesh,
        in_specs=(
            P(None, "ctx", "ch"), P(None, None, "ch"), P("ch", None), P("ch", None), P("ch"), P("ch", "ctx"),
        ),
        out_specs=P("ctx", "ch"),
        check_vma=False,
    )
```

```python
import functools

import jax
import jax.numpy as jnp
from jax import lax
from jax.experimental import pallas as pl
from jax.experimental.pallas import tpu as pltpu
from jax.sharding import PartitionSpec as P

MESH = pl.DeviceIdType.MESH
F32 = jnp.float32
BF16 = jnp.bfloat16
STEPS = 16
MODES = 16
OWN = 2
OTHER = 2
BLOCKS = 8


TURNS = (
    (-5, 4, 0, -4, 5, 1, -6, 6, -3, 2, -7, 7, -2, 3, -1, -8),
    (4, -5, 0, -4, 5, 1, -6, 6, 3, -1, 7, -7, -3, 2, -2, -8),
    (5, -4, 0, 4, -5, 1, 6, -6, 3, -1, 7, -7, -3, 2, -2, -8),
    (5, -4, 4, 0, -5, -1, 6, -6, 3, -2, 7, -7, 2, -3, 1, -8),
)


def kernel(
    proj_h, sfilt_h, res_h, dec_h, skip_h, wt, out,
    proj, sfilt, res, dec, skip,
    x32, lam_t, al_t, l16_t, l32_t, l64_t, l127_t, l126_t, cor_t, kv_t, taps_t, sf_t, l128_t, l2048_t, pow_t, z_t, q_t, u_t, y_t, gt,
    hal_s, hal_r, sb, ab, tb, bb, cs, cr, wbuf, gb, ps, rb,
    in_s, h_s, h_r, w_s, w_r, x2_r, xf_r, ph_s, ph_r, g_s, g_r, rs_s, rs_r, st,
):
    ctx = lax.axis_index("ctx")
    y = lax.axis_index("ch")
    z = ctx // 8
    x = (ctx // 2) % 4
    c = ctx % 2
    grp = ctx // 16
    g = ctx % 16
    sib = z * 8 + x * 2 + (1 - c)

    def at(zz, xx):
        return (zz % 16) * 8 + (xx % 4) * 2 + c

    zr, zl = at(z + 1, x), at(z + 15, x)
    xr, xl, xo = at(z, x + 1), at(z, x + 3), at(z, x + 2)
    nxt, prv = (ctx + 1) % 128, (ctx + 127) % 128

    me_slot = z * 4 + x

    barrier = pltpu.get_barrier_semaphore()
    twin = at(z + 1 - 2 * (z % 2) + 16, x)
    near = (zr, zl, xr, xl, xo, sib, prv, twin + 1 - 2 * c, at(z + 2, x), at(z + 14, x))
    for who in near:
        pl.semaphore_signal(barrier, inc=1, device_id=(who, y), device_id_type=MESH)
    for d in range(1, 4):
        pl.semaphore_signal(barrier, inc=1, device_id=(ctx, (y + d) % 4), device_id_type=MESH)

    def fetch(k, src, dst):
        return pltpu.make_async_copy(src, dst, in_s.at[k])

    fetches = [
        fetch(0, proj_h, proj), fetch(1, wt, wbuf.at[me_slot]), fetch(2, dec_h, dec),
        fetch(3, sfilt_h, sfilt), fetch(4, res_h, res), fetch(5, skip_h, skip),
    ]
    for copy in fetches:
        copy.start()

    row = lax.broadcasted_iota(jnp.int32, (8, 128), 0)
    chunk_start = row.astype(F32) * float(STEPS)
    pl.semaphore_wait(barrier, len(near) + 3)

    def tell(k, partners):
        for who in partners:
            pl.semaphore_signal(st.at[k], inc=1, device_id=(who, y), device_id_type=MESH)

    def halo_copy():
        return pltpu.make_async_remote_copy(
            src_ref=hal_s, dst_ref=hal_r, send_sem=h_s, recv_sem=h_r,
            device_id=(nxt, y), device_id_type=MESH)

    def rows_of(slot, part, parts):
        size = 32 // parts
        return wbuf.at[slot, pl.ds(part * size, size)]

    def push(slot, part, parts, who, sem):
        block = rows_of(slot, part, parts)
        pltpu.make_async_remote_copy(
            src_ref=block, dst_ref=block, send_sem=w_s, recv_sem=sem,
            device_id=(who, y), device_id_type=MESH).start()

    def landed(slot, part, parts, sem):
        block = rows_of(slot, part, parts)
        pltpu.make_async_copy(block, block, sem).wait()

    def spread(slot, offset, part):
        n = offset % 16
        push(slot, part, OWN, xr, xf_r.at[0, n, part])
        push(slot, part, OWN, xl, xf_r.at[1, n, part])

    def slot_of(offset, xx):
        return ((z + offset + 16) % 16) * 4 + (xx % 4)

    ways = ((-1, zr), (1, zl))

    def push_mine(part, parts, who, sem):
        size = 32 // parts
        pltpu.make_async_remote_copy(
            src_ref=wt.at[pl.ds(part * size, size)], dst_ref=rows_of(me_slot, part, parts),
            send_sem=w_s, recv_sem=sem, device_id=(who, y), device_id_type=MESH).start()

    for part in range(OWN):
        for way in range(2):
            push_mine(part, OWN, ways[way][1], w_r.at[way, 0, part])
    for part in range(OTHER):
        push_mine(part, OTHER, xo, x2_r.at[part])
    tell(0, (sib, xr, xl, xo, at(z + 2, x), at(z + 14, x)))

    fetches[0].wait()
    for b in range(3):
        rows = proj[b, 112:128, :].astype(F32)
        for l in range(BLOCKS):
            hal_s[l, 2 * b : 2 * b + 2, :] = rows[14:16, l * 128 : (l + 1) * 128]
    for l in range(BLOCKS):
        hal_s[l, 6:8, :] = jnp.zeros((2, 128), F32)
    halo_copy().start()

    def relay_own(k):
        for part in range(OWN):
            for way, (sign, onward) in enumerate(ways):
                last = 8 if part % 2 == way else 7
                if k <= last:
                    slot = slot_of(sign * k, x)
                    landed(slot, part, OWN, w_r.at[way, k - 1, part])
                    if k < last:
                        push(slot, part, OWN, onward, w_r.at[way, k, part])
            for way, (sign, _) in enumerate(ways):
                if k <= (8 if part % 2 == way else 7):
                    spread(slot_of(sign * k, x), sign * k, part)

    def relay_other(k):
        for part in range(OTHER):
            for way, (sign, onward) in enumerate(ways):
                last = 8 if part % 2 == way else 7
                if k <= last:
                    slot = slot_of(sign * k, x + 2)
                    landed(slot, part, OTHER, w_r.at[2 + way, k - 1, part])
                    if k < last:
                        push(slot, part, OTHER, onward, w_r.at[2 + way, k, part])

    for copy in fetches[1:]:
        copy.wait()
    for l in range(BLOCKS):
        lanes = slice(l * 128, (l + 1) * 128)
        for b in range(3):
            x32[b, l] = proj[b, :, lanes].astype(F32)
        rate = dec[:, lanes]
        lam_t[l] = jnp.exp(-rate)
        l16_t[l] = jnp.exp(-16.0 * rate)
        l32_t[l] = jnp.exp(-32.0 * rate)
        l64_t[l] = jnp.exp(-64.0 * rate)
        l127_t[l] = jnp.exp(-127.0 * rate)
        l126_t[l] = jnp.exp(-126.0 * rate)
        hop = jnp.exp(-128.0 * rate)
        far = jnp.exp(-2048.0 * rate)
        for half in range(2):
            l128_t[half * 8 + l] = hop[half * 8 : half * 8 + 8]
            l2048_t[half * 8 + l] = far[half * 8 : half * 8 + 8]
        for b in range(3):
            sf_t[l, 3 * b : 3 * b + 3, :] = sfilt[b, :, lanes]

    def tables(l, carry):
        rate = dec_block(l)
        lam = lam_t[l]
        amp = res_block(l) * jnp.sqrt(rate)
        al_t[l] = amp * lam
        weight = amp
        rows = []
        for tap in range(STEPS):
            rows.append(jnp.sum(weight, axis=0, keepdims=True))
            weight = weight * lam
        rows[0] = rows[0] + skip[:, pl.ds(pl.multiple_of(l * 128, 128), 128)]
        for tap in range(STEPS):
            taps_t[l, tap : tap + 1, :] = rows[tap]
        for m in range(MODES):
            pow_t[l, m] = jnp.exp(-chunk_start * rate[m : m + 1, :])
        return carry

    def dec_block(l):
        return dec[:, pl.ds(pl.multiple_of(l * 128, 128), 128)]

    def res_block(l):
        return res[:, pl.ds(pl.multiple_of(l * 128, 128), 128)]

    known = jnp.where(ctx == 0, 0.0, 1.0).astype(F32)
    keep1 = jnp.where(row >= 1, 1.0, 0.0).astype(F32)
    keep2 = jnp.where(row >= 2, 1.0, 0.0).astype(F32)
    keep4 = jnp.where(row >= 4, 1.0, 0.0).astype(F32)

    def states(l, carry):
        filt = sf_t[l]
        shorts = []
        for b in range(3):
            xs = [x32[b, l, pl.ds(j, 8, stride=STEPS), :] for j in range(STEPS)]
            before1 = pltpu.roll(xs[15], 1, 0) * keep1
            before2 = pltpu.roll(xs[14], 1, 0) * keep1
            line = [before2, before1] + xs
            f0, f1, f2 = (filt[3 * b + i : 3 * b + i + 1, :] for i in range(3))
            shorts.append([f0 * line[j + 2] + f1 * line[j + 1] + f2 * line[j] for j in range(STEPS)])
        us = [(shorts[1][j] * shorts[2][j]).astype(BF16).astype(F32) for j in range(STEPS)]
        for j in range(STEPS):
            q_t[l, j] = shorts[0][j]
            u_t[l, j] = us[j]
        for j in range(2):
            kv_t[l, j], kv_t[l, 2 + j] = shorts[1][j], shorts[2][j]
        lam, l16, l32, l64 = lam_t[l], l16_t[l], l32_t[l], l64_t[l]
        for m in range(MODES):
            rate = jnp.broadcast_to(lam[m : m + 1, :], (8, 128))
            end = us[0]
            for j in range(1, STEPS):
                end = end * rate + us[j]
            end = end + pltpu.roll(end, 1, 0) * (keep1 * l16[m : m + 1, :])
            end = end + pltpu.roll(end, 2, 0) * (keep2 * l32[m : m + 1, :])
            end = end + pltpu.roll(end, 4, 0) * (keep4 * l64[m : m + 1, :])
            z_t[l, m] = pltpu.roll(end, 1, 0) * keep1
            sb[(m // 8) * 8 + l, m % 8 : m % 8 + 1, :] = end[7:8, :]
        return carry

    first_row = jnp.where(row == 0, 1.0, 0.0).astype(F32) * known

    def join(l, carry):
        halo = hal_r[l]
        filt = sf_t[l]
        adds = []
        for b in range(3):
            old2, old1 = halo[2 * b : 2 * b + 1, :], halo[2 * b + 1 : 2 * b + 2, :]
            f1, f2 = (filt[3 * b + i : 3 * b + i + 1, :] for i in (1, 2))
            adds.append((first_row * (f1 * old1 + f2 * old2), first_row * (f2 * old1)))
        deltas = []
        for j in range(2):
            q_t[l, j] = q_t[l, j] + adds[0][j]
            u = ((kv_t[l, j] + adds[1][j]) * (kv_t[l, 2 + j] + adds[2][j])).astype(BF16).astype(F32)
            deltas.append((u - u_t[l, j])[0:1, :])
            u_t[l, j] = u
        end = l127_t[l] * deltas[0] + l126_t[l] * deltas[1]
        sb[l] = sb[l] + end[:8]
        sb[8 + l] = sb[8 + l] + end[8:]
        grow = jnp.exp(dec_block(l))
        cor_t[l] = grow * (deltas[0] + grow * deltas[1])
        return carry

    lax.fori_loop(0, 4, states, 0)
    other = slot_of(0, x + 2)
    for part in range(OTHER):
        landed(other, part, OTHER, x2_r.at[part])
        push(other, part, OTHER, zr, w_r.at[2, 0, part])
        push(other, part, OTHER, zl, w_r.at[3, 0, part])
    lax.fori_loop(4, 8, states, 0)
    relay_own(1)
    halo_copy().wait()
    lax.fori_loop(0, BLOCKS, join, 0)
    pl.semaphore_wait(st.at[0], 6)
    tell(1, (at(z + 4, x), at(z + 12, x)))

    def member(d):
        return (g + d) % 16

    def to_member(src, dst, d, k):
        pltpu.make_async_remote_copy(
            src_ref=src, dst_ref=dst, send_sem=ph_s.at[k], recv_sem=ph_r.at[k],
            device_id=(grp * 16 + member(d), y), device_id_type=MESH).start()

    ab[g] = sb[g]

    members = (4, 12, 5, 11, 3, 13, 8, 7, 9, 6, 10, 2, 14, 15, 1)
    for d in members:
        to_member(sb.at[member(d)], ab.at[g], d, 0)

    def local(l, carry):
        us = [u_t[l, j] for j in range(STEPS)]
        taps = taps_t[l]
        rows = [jnp.broadcast_to(taps[t : t + 1, :], (8, 128)) for t in range(STEPS)]
        for j in range(STEPS):
            total = rows[0] * us[j]
            for t in range(1, j + 1):
                total = total + rows[t] * us[j - t]
            y_t[l, j] = total
        return carry

    relay_other(1)
    lax.fori_loop(0, BLOCKS, tables, 0)
    relay_own(2)
    lax.fori_loop(0, 8, local, 0)
    relay_other(2)

    def group_wait(buf, count, k):
        part = buf.at[pl.ds(0, count)]
        pltpu.make_async_copy(part, part, ph_r.at[k]).wait()

    group_wait(ab, 15, 0)
    hop = l128_t[g]
    total = ab[0]
    for h in range(1, 16):
        total = total * hop + ab[h]
    tb[...] = total

    pl.semaphore_wait(st.at[1], 2)
    for d in (4, 3, 5, 2, 6, 1, 7):
        pltpu.make_async_remote_copy(
            src_ref=tb, dst_ref=bb.at[d - 1], send_sem=ph_s.at[1], recv_sem=ph_r.at[1],
            device_id=(((grp + d) % 8) * 16 + g, y), device_id_type=MESH).start()
    for part in range(OWN):
        push_mine(part, OWN, xr, xf_r.at[0, 0, part])
        push_mine(part, OWN, xl, xf_r.at[1, 0, part])
    relay_own(3)
    relay_other(3)
    relay_own(4)
    relay_other(4)
    group_wait(bb, 7, 1)
    far = l2048_t[g]
    state = jnp.zeros((8, 128), F32)
    for d in range(7, 0, -1):
        state = state * far + bb[d - 1] * jnp.where(grp >= d, 1.0, 0.0).astype(F32)
    for h in range(16):
        cs[h] = state
        state = state * hop + ab[h]
    cr[g] = cs[g]

    for d in members:
        to_member(cs.at[member(d)], cr.at[g], d, 2)
    relay_own(5)
    relay_other(5)
    group_wait(cr, 15, 2)

    def finish(l, carry):
        ys = [y_t[l, j] for j in range(STEPS)]
        lam, al, cor = lam_t[l], al_t[l], cor_t[l]
        tiles = [cr[l], cr[8 + l]]
        for m in range(MODES):
            rate = jnp.broadcast_to(lam[m : m + 1, :], (8, 128))
            start = z_t[l, m] + pow_t[l, m] * (tiles[m // 8][m % 8 : m % 8 + 1, :] + keep1 * cor[m : m + 1, :])
            term = start * al[m : m + 1, :]
            for j in range(STEPS):
                ys[j] = ys[j] + term
                if j < STEPS - 1:
                    term = term * rate
        for j in range(STEPS):
            gt[l, pl.ds(j, 8, stride=STEPS), :] = q_t[l, j] * ys[j]
        return carry

    def gated(half):
        lanes = pl.ds(half * 512, 512)
        return pltpu.make_async_remote_copy(
            src_ref=gb.at[0, :, lanes], dst_ref=gb.at[1, :, lanes], send_sem=g_s.at[half],
            recv_sem=g_r.at[half], device_id=(sib, y), device_id_type=MESH)

    for half in range(2):
        lax.fori_loop(4 * half, 4 * half + 4, finish, 0)
        for l in range(4 * half, 4 * half + 4):
            gb[0, :, l * 128 : (l + 1) * 128] = gt[l].astype(BF16)
        gated(half).start()
        if half == 0:
            relay_own(6)

    def distance(turn):
        a, b, c_, d = (row[turn] % 16 for row in TURNS)
        r = z % 4
        return jnp.where(r == 0, a, jnp.where(r == 1, b, jnp.where(r == 2, c_, d)))

    def units(*turns, cores=(0, 1)):
        weights = []
        for turn in turns:
            n = distance(turn)
            zq = (z + n) % 16
            if 0 in cores:
                for part in range(OWN):
                    landed(zq * 4 + (x + 3) % 4, part, OWN, xf_r.at[0, n, part])
                    landed(zq * 4 + (x + 1) % 4, part, OWN, xf_r.at[1, n, part])
            weights.append(wbuf[pl.ds(zq * 4, 4)].reshape(128, 1024))
        tokens = gb[cores[0] : cores[-1] + 1].reshape(128 * len(cores), 1024)
        part = lax.dot_general(
            tokens, jnp.concatenate(weights, axis=0), (((1,), (1,)), ((), ())),
            preferred_element_type=F32).astype(BF16)
        for i, turn in enumerate(turns):
            for k, core in enumerate(cores):
                ps[2 * turn + core] = part[k * 128 : (k + 1) * 128, i * 128 : (i + 1) * 128]
                ship(turn, (z + distance(turn)) % 16, core)

    def ship(n, zq, core):
        owner, place = zq // 4, zq % 4
        dy = (owner - y + 4) % 4

        def copy(who):
            pltpu.make_async_remote_copy(
                src_ref=ps.at[2 * n + core], dst_ref=rb.at[dy, core, place], send_sem=rs_s,
                recv_sem=rs_r.at[dy, core, place], device_id=(who, owner), device_id_type=MESH).start()

        if core == 1:
            copy(sib)
        else:
            @pl.when(dy != 0)
            def _():
                copy(ctx)

            @pl.when(dy == 0)
            def _():
                rb[0, 0, place] = ps[2 * n]

    units(0, 1, cores=(0,))
    units(2, 3, cores=(0,))
    for half in range(2):
        gated(half).wait()
    units(0, 1, cores=(1,))
    units(2, 3, cores=(1,))
    relay_other(6)
    units(4, 5)
    relay_own(7)
    units(6, 7)
    relay_other(7)
    units(8, 9)
    relay_own(8)
    units(10, 11)
    units(12, 13)
    units(14)
    relay_other(8)
    units(15)

    lane = lax.broadcasted_iota(jnp.int32, (128, 128), 1) // 32
    first = (4 * y - z + 16) % 16
    for turn in range(4):
        place = jnp.where(first < 8, turn, 3 - turn)
        sums = []
        for core in range(2):
            rel = (core + c) % 2
            for dy in range(4):
                if core == 0:
                    for r in range(2):
                        if dy or r:
                            pltpu.make_async_copy(
                                rb.at[dy, r, place], rb.at[dy, r, place], rs_r.at[dy, r, place]).wait()
            acc = rb[0, rel, place].astype(F32)
            for dy in range(1, 4):
                acc = acc + rb[dy, rel, place].astype(F32)
            sums.append(acc)
        a, b = sums

        def pick(parts):
            return jnp.where(lane == 0, parts[0], jnp.where(lane == 1, parts[1], jnp.where(lane == 2, parts[2], parts[3])))

        a32, a64, a96 = (pltpu.roll(a, s, 1) for s in (32, 64, 96))
        b32, b64, b96 = (pltpu.roll(b, s, 1) for s in (32, 64, 96))
        at0 = pl.multiple_of(place * 256, 128)
        out[:, pl.ds(at0, 128)] = pick((a, b32, a32, b64)).astype(BF16)
        out[:, pl.ds(pl.multiple_of(at0 + 128, 128), 128)] = pick((a64, b96, a96, b)).astype(BF16)

    part = wbuf.at[pl.ds(0, 63)]
    pltpu.make_async_copy(part, part, w_s).wait()
    for k, (buf, count) in enumerate(((sb, 15), (bb, 7), (cs, 15))):
        part = buf.at[pl.ds(0, count)]
        pltpu.make_async_copy(part, part, ph_s.at[k]).wait()
    part = ps.at[pl.ds(0, 28)]
    pltpu.make_async_copy(part, part, rs_s).wait()


def on_device(projected, short_filter, residues, decays, skip, out_weight):
    tile = (BLOCKS, MODES, 128)
    vm = pltpu.VMEM
    dma = pltpu.SemaphoreType.DMA
    return pl.pallas_call(
        kernel,
        out_shape=jax.ShapeDtypeStruct((128, 1024), BF16),
        in_specs=[pl.BlockSpec(memory_space=pl.ANY)] * 6,
        out_specs=pl.BlockSpec(memory_space=pltpu.VMEM),
        scratch_shapes=[
            vm((3, 128, 1024), BF16), vm((3, 3, 1024), F32), vm((16, 1024), F32), vm((16, 1024), F32), vm((1, 1024), F32),
            vm((3, 8, 128, 128), F32),
            vm(tile, F32), vm(tile, F32), vm(tile, F32), vm(tile, F32), vm(tile, F32),
            vm(tile, F32), vm(tile, F32), vm(tile, F32), vm((8, 4, 8, 128), F32), vm(tile, F32), vm(tile, F32),
            vm((16, 8, 128), F32), vm((16, 8, 128), F32),
            vm((8, 16, 8, 128), F32), vm((8, 16, 8, 128), F32),
            vm((8, 16, 8, 128), F32), vm((8, 16, 8, 128), F32), vm((8, 16, 8, 128), F32),
            vm((8, 128, 128), F32),
            vm((8, 8, 128), F32), vm((8, 8, 128), F32),
            vm((16, 8, 128), F32), vm((16, 8, 128), F32), vm((8, 128), F32),
            vm((8, 8, 128), F32), vm((16, 8, 128), F32), vm((16, 8, 128), F32),
            vm((64, 32, 1024), BF16), vm((2, 128, 1024), BF16),
            vm((32, 128, 128), BF16), vm((4, 2, 4, 128, 128), BF16),
            dma((6,)), dma, dma, dma, dma((4, 8, 2)), dma((2,)), dma((2, 16, 2)), dma((3,)), dma((3,)),
            dma((2,)), dma((2,)), dma, dma((4, 2, 4)), pltpu.SemaphoreType.REGULAR((2,)),
        ],
        compiler_params=pltpu.CompilerParams(
            collective_id=0, has_side_effects=True, vmem_limit_bytes=63 * 2**20),
        cost_estimate=pl.CostEstimate(flops=2**31, bytes_accessed=2**21, transcendentals=2**18),
        name="hyena",
    )(projected, short_filter, residues.T, decays.T, skip[None, :], out_weight.T)


def solution(mesh):
    return jax.shard_map(
        on_device,
        mesh=mesh,
        in_specs=(
            P(None, "ctx", "ch"), P(None, None, "ch"), P("ch", None), P("ch", None), P("ch"), P("ch", "ctx"),
        ),
        out_specs=P("ctx", "ch"),
        check_vma=False,
    )
```
